128 devices in a mesh: grp: 8 (over x_lo, y), tile: 16 (over z, x_hi, core).
Axes of the slice: x: 4 (x_hi: 2, x_lo: 2; x = x_hi * 2 + x_lo), y: 4, z: 4, core: 2. Of those that a mesh axis runs over, the one named last changes fastest.
Arguments:
- field: bfloat16 [256, 128, 16, 128], P('tile', 'grp'), may hold values from -6 to 6
- sea: int32 [256, 128, 16], P('tile', 'grp'), may hold values 0 or 1
- conv_weight: bfloat16 [3, 3, 3, 128, 128], replicated, may hold values from -0.109375 to 0.109375
- lift_weight: bfloat16 [128, 1024], replicated, may hold values from -0.5 to 0.5
- mix_weight: bfloat16 [2, 1024, 1024], P(None, 'grp'), may hold values from -0.125 to 0.125
- proj_weight: bfloat16 [1024, 128], replicated, may hold values from -0.1875 to 0.1875
- kx_modes: int32 [32], replicated, may hold values from 0 to 127, as said below
- ky_modes: int32 [32], replicated, may hold values from 0 to 63, as said below
- kz_modes: int32 [4], replicated, may hold values from 0 to 7, as said below
- cotangent: bfloat16 [256, 128, 16, 128], P('tile', 'grp'), may hold values from -0.03125 to 0.03125
Outputs:
- output_cells: bfloat16 [256, 128, 16, 128], P('tile', 'grp')
- grad_conv: float32 [3, 3, 3, 128, 128], replicated
- grad_lift: float32 [128, 1024], replicated
- grad_mix: float32 [2, 1024, 1024], P(None, 'grp')
- grad_proj: float32 [1024, 128], replicated
The draws below stay inside these ranges and needn't reach their ends.
Inputs may be any that keep to these rules, and one draw needn't show every extreme that they name: `kx_modes`: 32 distinct frequencies, 0 and 127 among them. `ky_modes`: 32 distinct frequencies, 0 and 63 among them. `kz_modes`: 4 distinct frequencies, 0 and 7 among them.
All inputs are finite; a program needn't handle non-finite values. No bound on the sum of `sea` on one device may be relied on, other than what follows from the above.
Results may differ from the reference program's by a relative error of at most 0.03.
Values may be sent and summed in bfloat16 or wider, within the bound.
A program may use at most 128 MiB of HBM per device.

```python
import math
import jax
import jax.numpy as jnp
from jax import lax

C = 128
W = 1024
BX = 128
BY = 64
BZ = 8
KX = 32
KY = 32
KZ = 4
NX = 256
NY = 128
NZ = 16


def choose_modes(key, length, count):
    inner = jax.random.permutation(jax.random.fold_in(key, 11), length - 2) + 1
    ends = jnp.array([0, length - 1], dtype=jnp.int32)
    chosen = jnp.concatenate([ends, inner[:count - 2].astype(jnp.int32)])
    return jax.random.permutation(jax.random.fold_in(key, 12), chosen).astype(jnp.int32)


def draw_kx_modes(key, part):
    key = jax.random.fold_in(key, 1)
    return choose_modes(key, BX, KX)


def draw_ky_modes(key, part):
    key = jax.random.fold_in(key, 2)
    return choose_modes(key, BY, KY)


def draw_kz_modes(key, part):
    key = jax.random.fold_in(key, 3)
    return choose_modes(key, BZ, KZ)


def with_ends(result, key, smallest, high):
    longest = result.shape.index(max(result.shape))
    spots = []
    for shift in (0, 1):
        where = [jax.random.randint(jax.random.fold_in(key, axis), (), 0, length) for axis, length in enumerate(result.shape)]
        where[longest] = (where[longest] + shift) % result.shape[longest]
        spots.append(tuple(where))
    return result.at[spots[0]].set(smallest).at[spots[1]].set(high)


def block_levels(key, shape, shards, smallest, high):
    def one(axis_at, blocks):
        heights = jax.random.uniform(jax.random.fold_in(jax.random.fold_in(key, 6), axis_at), (blocks,), jnp.float32, smallest / len(shards), high / len(shards))
        return jnp.repeat(jnp.exp(heights), shape[axis_at] // blocks).reshape((-1,) + (1,) * (len(shape) - axis_at - 1))

    gain = one(*shards[0])
    for cut in shards[1:]:
        gain = gain * one(*cut)
    return gain


def scatter_about(stream_key, dims, scale, most, cuts=(), held_as=jnp.bfloat16):
    values = jax.random.normal(stream_key, dims, jnp.float32) * scale
    if len(cuts) > 0:
        values = block_levels(stream_key, dims, cuts, -0.22, 0.18) * values
    return jnp.clip(values, min=-most, max=most).astype(held_as)


def setup_inputs(seed: int = 0) -> dict:
    splits = jax.random.split(jax.random.key(seed), 11)
    return {
        "field": scatter_about(splits[0], (NX, NY, NZ, C), 1.0, 6.0, ((0, 16), (1, 8))),
        "sea": with_ends((jax.random.randint(splits[1], (NX, NY, NZ), 0, 4) < 3).astype(jnp.int32), jax.random.fold_in(splits[1], 1), 0, 1),
        "conv_weight": scatter_about(splits[2], (3, 3, 3, C, C), (27 * C) ** -0.5, 0.109375),
        "lift_weight": scatter_about(splits[3], (C, W), C ** -0.5, 0.5),
        "mix_weight": scatter_about(splits[4], (2, W, W), (2 * W) ** -0.5, 0.125, ((1, 8),)),
        "proj_weight": scatter_about(splits[5], (W, C), W ** -0.5, 0.1875),
        "kx_modes": draw_kx_modes(jax.random.fold_in(splits[10], 71), 0),
        "ky_modes": draw_ky_modes(jax.random.fold_in(splits[10], 71), 0),
        "kz_modes": draw_kz_modes(jax.random.fold_in(splits[10], 71), 0),
        "cotangent": scatter_about(splits[9], (NX, NY, NZ, C), (4.0 * (NX * NY * NZ) ** -0.5), 0.03125, ((0, 16), (1, 8))),
    }


def widen(values):
    return values.astype(jnp.float32)

def phase_angles(freq_list, length):
    positions = jnp.arange(length, dtype=jnp.int32)
    turn_count = freq_list.astype(jnp.int32)[:, None] * positions[None, :] % length
    return turn_count.astype(jnp.float32) * (2.0 * math.pi / length)

def make_plane(ky_modes, kz_modes):
    angles = phase_angles(ky_modes, BY)[:, None, :, None] + phase_angles(kz_modes, BZ)[None, :, None, :]
    result_table = jnp.stack([jnp.cos(angles), -jnp.sin(angles)], 0)
    return result_table.reshape(2 * KY * KZ, BY * BZ).astype(jnp.bfloat16)

def make_line(kx_modes):
    angles = phase_angles(kx_modes, BX)
    cosine = jnp.cos(angles)
    sine_vals = jnp.sin(angles)
    upper_rows = jnp.stack([cosine, sine_vals], 1)
    lower_rows = jnp.stack([-sine_vals, cosine], 1)
    return jnp.stack([upper_rows, lower_rows], 0).astype(jnp.bfloat16)

def conv_cells(padded, conv_weight, extent):
    size_x, size_y, size_z = extent
    summed = None
    for shift_x in range(3):
        for shift_y in range(3):
            stacked = jnp.concatenate([padded[shift_x:shift_x + size_x, shift_y:shift_y + size_y, shift_z:shift_z + size_z] for shift_z in range(3)], -1)
            weights = conv_weight[shift_x, shift_y].reshape(-1, conv_weight.shape[-1])
            product = jnp.dot(stacked.reshape(-1, weights.shape[0]), weights, preferred_element_type=jnp.float32)
            summed = product if summed is None else summed + product
    return summed

def conv_grads(padded, grad_rows, extent):
    size_x, size_y, size_z = extent
    channels = padded.shape[-1]
    pieces = []
    for shift_x in range(3):
        for shift_y in range(3):
            stacked = jnp.concatenate([padded[shift_x:shift_x + size_x, shift_y:shift_y + size_y, shift_z:shift_z + size_z] for shift_z in range(3)], -1)
            pieces.append(lax.dot_general(stacked.reshape(-1, 3 * channels), grad_rows, (((0,), (0,)), ((), ())), preferred_element_type=jnp.float32))
    return jnp.stack(pieces).reshape(3, 3, 3, channels, grad_rows.shape[-1])

def block_mean(values):
    rows_x, rows_y, rows_z, channels = values.shape
    return widen(values).reshape(rows_x // 2, 2, rows_y // 2, 2, rows_z // 2, 2, channels).mean(axis=(1, 3, 5))

def block_sum(values):
    rows_x, rows_y, rows_z, channels = values.shape
    return values.reshape(rows_x // 2, 2, rows_y // 2, 2, rows_z // 2, 2, channels).sum(axis=(1, 3, 5))

def spread_blocks(values):
    rows_x, rows_y, rows_z, channels = values.shape
    spread = jnp.broadcast_to(values[:, None, :, None, :, None, :], (rows_x, 2, rows_y, 2, rows_z, 2, channels))
    return spread.reshape(2 * rows_x, 2 * rows_y, 2 * rows_z, channels)

def gelu_back(inputs, upstream):
    return jax.vjp(jax.nn.gelu, inputs)[1](upstream)[0]

def left_dot(first, second):
    return lax.dot_general(first, second, (((0,), (0,)), ((), ())), preferred_element_type=jnp.float32)

def right_dot(first, second):
    return lax.dot_general(first, second, (((1,), (1,)), ((), ())), preferred_element_type=jnp.float32)

def forward_modes(cell_vals, plane_tab, line_tab):
    partial_sum = jnp.einsum('kn,xnw->xkw', widen(plane_tab), widen(cell_vals)).astype(jnp.bfloat16)
    flat_part = partial_sum.reshape(BX, 2, -1)
    mode_vals = jnp.einsum('qkpx,xpr->qkr', widen(line_tab), widen(flat_part)).astype(jnp.bfloat16)
    return mode_vals.reshape(2, KX * KY * KZ, cell_vals.shape[2])

def adjoint_cells(mode_vals, plane_tab, line_tab):
    flat_modes = mode_vals.reshape(2, KX, -1)
    inverse = jnp.einsum('qkpx,qkr->xpr', widen(line_tab), widen(flat_modes)).astype(jnp.bfloat16)
    inverse = inverse.reshape(BX, 2 * KY * KZ, mode_vals.shape[2])
    return jnp.einsum('kn,xkw->xnw', widen(plane_tab), widen(inverse))

def reference(field, sea, conv_weight, lift_weight, mix_weight, proj_weight, kx_modes, ky_modes, kz_modes, cotangent):
    sea_cells = sea.astype(jnp.bfloat16)[..., None]
    masked = field * sea_cells
    padded = jnp.pad(masked, ((1, 1), (1, 1), (1, 1), (0, 0)))
    extent = (NX, NY, NZ)
    hidden_pre = conv_cells(padded, conv_weight, extent)
    hidden = jax.nn.gelu(hidden_pre).astype(jnp.bfloat16).reshape(NX, NY, NZ, C)
    coarse = block_mean(hidden).astype(jnp.bfloat16)
    coarse_rows = coarse.reshape(-1, C)
    lifted = jnp.dot(coarse_rows, lift_weight, preferred_element_type=jnp.float32).astype(jnp.bfloat16)
    lifted = lifted.reshape(BX, BY * BZ, W)
    plane_tab = make_plane(ky_modes, kz_modes)
    line_tab = make_line(kx_modes)
    spec_scale = 1.0 / math.sqrt(BX * BY * BZ * KX * KY * KZ)
    modes_in = forward_modes(lifted, plane_tab, line_tab)
    real_w = mix_weight[0]
    imag_w = mix_weight[1]
    mixed_real = jnp.dot(modes_in[0], real_w, preferred_element_type=jnp.float32) - jnp.dot(modes_in[1], imag_w, preferred_element_type=jnp.float32)
    mixed_imag = jnp.dot(modes_in[0], imag_w, preferred_element_type=jnp.float32) + jnp.dot(modes_in[1], real_w, preferred_element_type=jnp.float32)
    mixed = jnp.stack([mixed_real, mixed_imag]).astype(jnp.bfloat16)
    bottle_pre = spec_scale * adjoint_cells(mixed, plane_tab, line_tab) + widen(lifted)
    bottle = jax.nn.gelu(bottle_pre).astype(jnp.bfloat16)
    bottle_rows = bottle.reshape(-1, W)
    projected = jnp.dot(bottle_rows, proj_weight, preferred_element_type=jnp.float32).reshape(BX, BY, BZ, C)
    output_cells = ((widen(hidden) + spread_blocks(projected)) * widen(sea_cells)).astype(jnp.bfloat16)
    out_grad = widen(cotangent) * widen(sea_cells)
    proj_grad = block_sum(out_grad).astype(jnp.bfloat16).reshape(-1, C)
    grad_proj = left_dot(bottle_rows, proj_grad)
    bottle_grad = right_dot(proj_grad, proj_weight).astype(jnp.bfloat16)
    bottle_pre_grad = gelu_back(bottle_pre, widen(bottle_grad).reshape(bottle_pre.shape))
    space_grad = (spec_scale * bottle_pre_grad).astype(jnp.bfloat16)
    mixed_grad = forward_modes(space_grad, plane_tab, line_tab)
    grad_real = left_dot(modes_in[0], mixed_grad[0]) + left_dot(modes_in[1], mixed_grad[1])
    grad_imag = left_dot(modes_in[0], mixed_grad[1]) - left_dot(modes_in[1], mixed_grad[0])
    grad_mix = jnp.stack([grad_real, grad_imag])
    modes_real = right_dot(mixed_grad[0], real_w) + right_dot(mixed_grad[1], imag_w)
    modes_imag = right_dot(mixed_grad[1], real_w) - right_dot(mixed_grad[0], imag_w)
    modes_grad = jnp.stack([modes_real, modes_imag]).astype(jnp.bfloat16)
    lifted_grad = (bottle_pre_grad + adjoint_cells(modes_grad, plane_tab, line_tab)).astype(jnp.bfloat16)
    lifted_rows = lifted_grad.reshape(-1, W)
    coarse_grad = right_dot(lifted_rows, lift_weight)
    grad_lift = left_dot(coarse_rows, lifted_rows)
    hidden_grad = out_grad + 0.125 * spread_blocks(coarse_grad.reshape(BX, BY, BZ, C))
    hidden_pre_grad = gelu_back(hidden_pre, hidden_grad.reshape(-1, C)).astype(jnp.bfloat16)
    grad_conv = conv_grads(padded, hidden_pre_grad, extent)
    return (output_cells, grad_conv, grad_lift, grad_mix, grad_proj)
```

```python
import math

import jax
import jax.numpy as jnp
from jax import lax
from jax.experimental import pallas as pl
from jax.experimental.pallas import tpu as pltpu
from jax.sharding import PartitionSpec as P

BX = 128
BY = 64
BZ = 8
KX = 32
KY = 32
KZ = 4
C = 128
W = 1024
GRP = 8
TILE = 16
PAIRS = 8
SCALE = 1.0 / math.sqrt(BX * BY * BZ * KX * KY * KZ)
ROOT = math.sqrt(2.0 / math.pi)
CUBE = 0.044715
F32 = jnp.float32
BF16 = jnp.bfloat16
MESH = pl.DeviceIdType.MESH


def dot(first, second, left=1, right=0):
    return lax.dot_general(
        first, second, (((left,), (right,)), ((), ())), preferred_element_type=F32
    )


def grid_of(shape, dim):
    return lax.broadcasted_iota(jnp.int32, shape, dim)


def cos_sin(turns, length):
    angles = (turns & (length - 1)).astype(F32) * (2.0 * math.pi / length)
    return jnp.cos(angles), jnp.sin(angles)


def z_table(kz):
    shape = (64, 128)
    row, lane = grid_of(shape, 0), grid_of(shape, 1)
    freq = jnp.concatenate([jnp.full((16, 128), kz[b], jnp.int32) for b in range(KZ)], 0)
    cosine, sine = cos_sin(freq * (lane & 7), BZ)
    p, s = (row >> 3) & 1, lane >> 6
    value = jnp.where(s == p, jnp.where(s == 0, cosine, -cosine), -sine)
    return jnp.where((row & 7) == ((lane >> 3) & 7), value, 0.0)


def y_table(ky, first):
    shape = (32, 128)
    row, lane = grid_of(shape, 0), grid_of(shape, 1)
    freq = jnp.zeros(shape, jnp.int32)
    for a in range(16):
        freq = jnp.where((row >> 1) == a, ky[first + a], freq)
    y = ((lane >> 4) << 3) + (lane & 7)
    cosine, sine = cos_sin(freq * y, BY)
    p, q = (lane >> 3) & 1, row & 1
    return jnp.where(p == q, cosine, jnp.where(q == 0, sine, -sine))


def x_table(kx):
    shape = (32, 256)
    row, lane = grid_of(shape, 0), grid_of(shape, 1)
    freq = jnp.zeros(shape, jnp.int32)
    for k in range(KX):
        freq = jnp.where(row == k, kx[k], freq)
    x = ((lane >> 4) << 3) + (lane & 7)
    cosine, sine = cos_sin(freq * x, BX)
    even = ((lane >> 3) & 1) == 0
    return jnp.concatenate(
        [jnp.where(even, cosine, sine), jnp.where(even, -sine, cosine)], 0
    )


def spot(axis):
    return lax.axis_index(axis)


def place():
    grp, tile = spot("grp"), spot("tile")
    return {
        "xlo": grp // 4,
        "y": lax.rem(grp, 4),
        "z": tile // 4,
        "xhi": lax.rem(tile // 2, 2),
        "core": lax.rem(tile, 2),
    }


LENGTHS = {"xlo": 2, "y": 4, "z": 4, "xhi": 2, "core": 2}
DIGITS = {"ring_y": ("y",), "ring_z": ("z",), "xz": ("xlo", "z", "xhi"), "xy": ("xlo", "y", "xhi")}


def digits_of(name, number):
    digits = {}
    for part in reversed(DIGITS[name]):
        digits[part] = number % LENGTHS[part]
        number //= LENGTHS[part]
    return digits


def own(name):
    if name not in DIGITS:
        return spot(name)
    here = place()
    index = 0
    for part in DIGITS[name]:
        index = index * LENGTHS[part] + here[part]
    return index


def group(name):
    if name not in DIGITS:
        count = GRP if name == "grp" else TILE
        for away in range(1, count):
            index = lax.rem(spot(name) + away, count)
            yield away, index, {name: index}
        return
    count = math.prod(LENGTHS[part] for part in DIGITS[name])
    for away in range(1, count):
        there = place()
        index = 0
        for part, step in digits_of(name, away).items():
            if step:
                there[part] = lax.rem(there[part] + step, LENGTHS[part])
        for part in DIGITS[name]:
            index = index * LENGTHS[part] + there[part]
        device = {
            "grp": there["xlo"] * 4 + there["y"],
            "tile": there["z"] * 4 + there["xhi"] * 2 + there["core"],
        }
        yield away, index, device


def partner():
    tile = spot("tile")
    return {"tile": tile + 1 - 2 * lax.rem(tile, 2)}


def near(step_tile, step_grp):
    target = {}
    if step_tile:
        target["tile"] = lax.rem(spot("tile") + step_tile + TILE, TILE)
    if step_grp:
        target["grp"] = lax.rem(spot("grp") + step_grp + GRP, GRP)
    return target


DIAGONALS = ((1, 1), (1, -1), (-1, 1), (-1, -1))


def greet():
    barrier = pltpu.get_barrier_semaphore()
    targets = [device for name in ("grp", "tile") for _, _, device in group(name)]
    targets += [near(*step) for step in DIAGONALS]
    for away, _, device in group("xz"):
        steps = digits_of("xz", away)
        if steps["xlo"] and (steps["z"] or steps["xhi"]):
            targets.append(device)
    for away, _, device in group("xy"):
        steps = digits_of("xy", away)
        if steps["xhi"] and steps["y"]:
            targets.append(device)
    for device in targets:
        pl.semaphore_signal(barrier, inc=1, device_id=device, device_id_type=MESH)
    return lambda: pl.semaphore_wait(barrier, len(targets))


def remote(src, dst, sems, place, device):
    copy = pltpu.make_async_remote_copy(
        src_ref=src,
        dst_ref=dst,
        send_sem=sems.at[0, place],
        recv_sem=sems.at[1, place],
        device_id=device,
        device_id_type=MESH,
    )
    copy.start()
    return copy


def scatter_rows(src, slots, sems, name):
    return [
        remote(src.at[index], slots.at[away], sems, away, device)
        for away, index, device in group(name)
    ]


def add_rows(src, slots, copies, name):
    total = src[own(name)].astype(F32)
    for place, copy in enumerate(copies):
        copy.wait_recv()
        total += slots[place + 1].astype(F32)
    return total.astype(BF16)


def exchange(src, dst, sems, name):
    me = own(name)
    copies = [
        remote(src.at[index], dst.at[me], sems, away, device) for away, index, device in group(name)
    ]
    dst[me] = src[me]
    return copies


def spread_rows(src, dst, sems, name):
    me = own(name)
    copies = [remote(src, dst.at[me], sems, away, device) for away, index, device in group(name)]
    dst[me] = src[...]
    return copies


def arrived(copies):
    for copy in copies:
        copy.wait_recv()


def left(copies):
    for copy in copies:
        copy.wait_send()


def pair_sems(count):
    return pltpu.SemaphoreType.DMA((2, count))


def held(*shape, dtype=BF16):
    return pltpu.VMEM(shape, dtype)


FILTER_SCRATCH = (
    lambda: [held(KZ, 8, 16, C)]
    + [held(GRP, 8, 16, C) for _ in range(3)]
    + [held(TILE, 16, C) for _ in range(4)]
    + [held(256, C, dtype=F32)]
    + [pair_sems(GRP), pair_sems(TILE), pair_sems(TILE), pair_sems(GRP)]
)


def x_filter(y_tab, x_tab, work, beside):
    part, got_y, sent, back, mid, got, turned, home, wide, sem1, sem2, sem3, sem4 = work
    me = spot("grp")
    first = [
        remote(part.at[index // 2], got_y.at[me], sem1, away, device)
        for away, index, device in group("grp")
    ]
    got_y[me] = part[me // 2]
    beside[0]()
    arrived(first)
    for x in range(8):
        rows = got_y[:, x].reshape(128, C)
        wide[pl.ds(x, 32, stride=8), :] = dot(y_tab[...], rows)
    mid[...] = wide[...].astype(BF16).reshape(mid.shape)
    second = exchange(mid, got, sem2, "tile")
    beside[1]()
    arrived(second)
    modes = dot(x_tab[...], got[...].reshape(TILE * 16, C)).astype(BF16)
    turned[...] = dot(x_tab[...], modes, 0, 0).astype(BF16).reshape(turned.shape)
    third = exchange(turned, home, sem3, "tile")
    beside[2]()
    arrived(third)
    wide[...] = home[...].reshape(256, C).astype(F32)
    for x in range(8):
        rows = wide[pl.ds(x, 32, stride=8), :].astype(BF16)
        sent[:, x] = dot(y_tab[...], rows, 0, 0).astype(BF16).reshape(GRP, 16, C)
    fourth = exchange(sent, back, sem4, "grp")
    beside[3]()
    arrived(fourth)
    for copies in (first, second, third, fourth):
        left(copies)


SUM_SCRATCH = (
    lambda: [held(2, 4, 16, 16, C) for _ in range(2)]
    + [held(4, 16, 16, C) for _ in range(2)]
    + [held(16, 16, C) for _ in range(4)]
    + [held(16, C) for _ in range(2)]
    + [held(16, 16, C) for _ in range(2)]
    + [pair_sems(16) for _ in range(10)]
)


class Sums:
    def __init__(self, x, y, work):
        self.x, self.y = x, y
        self.buffers, self.sems = work[:12], work[12:]
        self.sent = []

    def run(self, step):
        x, y, s = self.x, self.y, self.sems
        got, mine, sa, sb, ma, mb, ra, rb, ta, tb, ga, gb = self.buffers
        core = place()["core"]
        if step == 0:
            self.a = [remote(x.at[1 - core], got, s[0], 0, partner())]
            self.b = []
        if step == 1:
            arrived(self.a)
            mine[...] = (x[core].astype(F32) + got[...].astype(F32)).astype(BF16)
            self.a = scatter_rows(mine.at[0], sa, s[1], "ring_y")
            self.b = scatter_rows(mine.at[1], sb, s[2], "ring_z")
        if step == 2:
            ma[...] = add_rows(mine.at[0], sa, self.a, "ring_y")
            self.a = scatter_rows(ma, ra, s[3], "xz")
            mb[...] = add_rows(mine.at[1], sb, self.b, "ring_z")
            self.b = scatter_rows(mb, rb, s[4], "xy")
        if step == 3:
            ta[...] = add_rows(ma, ra, self.a, "xz")
            self.a = spread_rows(ta, ga, s[5], "xz")
            tb[...] = add_rows(mb, rb, self.b, "xy")
            self.b = spread_rows(tb, gb, s[6], "xy")
        if step == 4:
            arrived(self.a)
            self.a = spread_rows(ga, y.at[core, 0], s[7], "ring_y")
            arrived(self.b)
            self.b = spread_rows(gb, y.at[core, 1], s[8], "ring_z")
        if step == 5:
            arrived(self.a)
            arrived(self.b)
            self.a = [remote(y.at[core], y.at[core], s[9], 0, partner())]
            self.b = []
        if step == 6:
            arrived(self.a)
            for copies in self.sent:
                left(copies)
            return
        self.sent += [self.a, self.b]


def block_at(n):
    return n // 16, n // 8 % 2, n % 8 // 2, pl.ds(8 * (n % 2), 8)


def tanh_of(x):
    return jnp.tanh(ROOT * (x + CUBE * x * x * x))


def gelu_slope(x, t):
    return 0.5 * (1.0 + t) + 0.5 * x * (1.0 - t * t) * (ROOT * (1.0 + 3.0 * CUBE * x * x))


def shift_rows(rows, forward):
    z = lax.rem(lax.broadcasted_iota(jnp.int32, rows.shape, 0), 16)
    if forward:
        return jnp.where(z == 0, 0.0, pltpu.roll(rows, 1, 0))
    return jnp.where(z == 15, 0.0, pltpu.roll(rows, rows.shape[0] - 1, 0))


def pool(rows, tmp):
    tmp[...] = rows.reshape(8, 2, 16, C).sum(1).reshape(128, C)
    return tmp[pl.ds(0, 64, stride=2), :] + tmp[pl.ds(1, 64, stride=2), :]


def unpool(rows, tmp):
    tmp[pl.ds(0, 64, stride=2), :] = rows
    tmp[pl.ds(1, 64, stride=2), :] = rows
    wide = jnp.broadcast_to(tmp[...].reshape(8, 1, 16, C), (8, 2, 16, C))
    return wide.reshape(256, C)


def step_kernel(
    field_in,
    sea_in,
    cot_in,
    conv_in,
    lift_in,
    mix_in,
    proj_in,
    kx,
    ky,
    kz,
    out,
    sums,
    taps,
    lift_parts,
    field,
    sea,
    cot,
    conv_w,
    lift,
    mix,
    proj,
    load_sems,
    x_tab,
    y_tab,
    z_tab,
    z_cells,
    z_twice,
    rim,
    rim_t,
    halo_x,
    halo_y,
    halo_c,
    conv_flat,
    pre,
    hidden,
    feats,
    proj_grad,
    lift_own,
    lm_part,
    lm_slots,
    lm_mine,
    lm_all,
    stacked,
    bottle_pre,
    bottle_grad,
    bottle,
    bpg,
    direct,
    cell_grad,
    acc,
    sums_in,
    taps_in,
    lift_mine,
    tmp,
    sem_halo,
    sem_lm1,
    sem_lm2,
    sem_lm3,
    sem_lift,
    *work,
):
    count = len(FILTER_SCRATCH())
    filter1, filter2 = work[:count], work[count : 2 * count]
    work = work[2 * count :]
    count = len(SUM_SCRATCH())
    first_sums = Sums(sums_in, sums, work[:count])
    last_sums = Sums(taps_in, taps, work[count:])
    grp, tile = spot("grp"), spot("tile")
    core = place()["core"]
    loads = []
    for i, (src, dst) in enumerate(
        (
            (field_in, field),
            (sea_in, sea),
            (conv_in, conv_w),
            (lift_in, lift),
            (mix_in, mix),
            (cot_in, cot),
            (proj_in, proj),
        )
    ):
        loads.append(pltpu.make_async_copy(src, dst, load_sems.at[i]))
        loads[i].start()
    met = greet()
    for copy in loads[:2]:
        copy.wait()

    @pl.loop(0, 16)
    def _(x):
        rim[x + 1, 1:17] = field[x] * sea[x]

    met()

    inner = pl.ds(1, 16)
    halos = [
        remote(rim.at[16, inner], halo_x.at[0], sem_halo, 0, near(1, 0)),
        remote(rim.at[1, inner], halo_x.at[1], sem_halo, 1, near(-1, 0)),
        remote(rim.at[inner, 16], halo_y.at[0], sem_halo, 2, near(0, 1)),
        remote(rim.at[inner, 1], halo_y.at[1], sem_halo, 3, near(0, -1)),
        remote(rim.at[16, 16], halo_c.at[0], sem_halo, 4, near(1, 1)),
        remote(rim.at[16, 1], halo_c.at[1], sem_halo, 5, near(1, -1)),
        remote(rim.at[1, 16], halo_c.at[2], sem_halo, 6, near(-1, 1)),
        remote(rim.at[1, 1], halo_c.at[3], sem_halo, 7, near(-1, -1)),
    ]
    for copy in loads[2:]:
        copy.wait()
    lift_own[...] = lift[:, pl.ds(pl.multiple_of(grp * C, C), C)]
    product = dot(lift_own[...], mix[core]).astype(BF16)
    for j in range(GRP):
        lm_part[j] = product[:, C * j : C * (j + 1)]

    for a in range(3):
        for b in range(3):
            for c in range(3):
                conv_flat[pl.ds(C * (3 * a + b), C), pl.ds(C * c, C)] = conv_w[a, b, c]

    @pl.loop(0, 8)
    def _(i):
        total = cot[2 * i].astype(F32) * sea[2 * i].astype(F32)
        total += cot[2 * i + 1].astype(F32) * sea[2 * i + 1].astype(F32)
        rows = pool(total.reshape(256, C), tmp)
        proj_grad[pl.ds(pl.multiple_of(64 * i, 64), 64), :] = rows.astype(BF16)

    stacked[pl.ds(0, C), :] = lift[...]
    x_tab[...] = x_table(kx).astype(BF16)
    y_tab[...] = y_table(ky, 16 * lax.rem(grp, 2)).astype(BF16)
    z_values = z_table(kz).astype(BF16)
    z_tab[...] = z_values
    z_cells[...] = z_values[:, :64]
    for j in range(GRP):
        z_twice[pl.ds(16 * j, 16), :] = z_values[16 * (j // 2) : 16 * (j // 2 + 1)]

    arrived(halos)
    lm_first = scatter_rows(lm_part, lm_slots, sem_lm1, "grp")
    sides = (tile > 0, tile < TILE - 1, grp > 0, grp < GRP - 1)

    def keep(flag, rows):
        return jnp.where(flag, rows, jnp.zeros_like(rows))

    for side, x in ((0, 0), (1, 17)):
        rim[x, 1:17] = keep(sides[side], halo_x[side])
    for side, y in ((0, 0), (1, 17)):
        rim[1:17, y] = keep(sides[2 + side], halo_y[side])
    for i, x, y in ((0, 0, 0), (1, 0, 17), (2, 17, 0), (3, 17, 17)):
        flag = jnp.logical_and(sides[0 if x == 0 else 1], sides[2 if y == 0 else 3])
        rim[x, y] = keep(flag, halo_c[i])

    def convolve(x):
        window = jnp.concatenate(
            [rim[x + a, b : b + 16].reshape(256, C) for a in range(3) for b in range(3)], 1
        )
        product = dot(window, conv_flat[...])
        rows = (
            product[:, C : 2 * C]
            + shift_rows(product[:, :C], True)
            + shift_rows(product[:, 2 * C :], False)
        )
        pre[x] = rows
        hidden[x] = (0.5 * rows * (1.0 + tanh_of(rows))).astype(BF16)

    pl.loop(0, 16)(convolve)

    for i in range(8):
        total = hidden[2 * i].astype(F32) + hidden[2 * i + 1].astype(F32)
        coarse = (0.125 * pool(total, tmp)).astype(BF16)
        feats[pl.ds(64 * i, 64), pl.ds(0, C)] = coarse
        filter1[0][:, i] = dot(z_cells[...], coarse).astype(BF16).reshape(KZ, 16, C)

    def turn_windows():
        @pl.loop(0, 18)
        def _(x):
            for b in range(3):
                rim_t[x, pl.ds(C * b, C), :] = rim[x, b : b + 16].reshape(256, C).T

    def back_through():
        for j in range(4):
            cols = pl.ds(256 * j, 256)
            bottle_grad[:, cols] = dot(proj_grad[...], proj[cols, :], 1, 1).astype(BF16)

    lm = {}

    def gather_lm():
        lm_mine[...] = add_rows(lm_part, lm_slots, lm_first, "grp")
        lm["grp"] = spread_rows(lm_mine, lm_all.at[core], sem_lm2, "grp")
        back_through()

    def swap_lm():
        arrived(lm["grp"])
        lm["core"] = [remote(lm_all.at[core], lm_all.at[core], sem_lm3, 0, partner())]

    x_filter(y_tab, x_tab, filter1, (turn_windows, gather_lm, lambda: None, swap_lm))

    arrived(lm["core"])
    for p in range(2):
        for j in range(GRP):
            stacked[pl.ds(C * (p + 1), C), pl.ds(C * j, C)] = lm_all[p, j]
    for copies in (lm_first, lm["grp"], lm["core"]):
        left(copies)

    for i in range(8):
        modes = filter1[3][:, i].reshape(128, C)
        both = (SCALE * dot(z_twice[...], modes, 0, 0)).astype(BF16)
        feats[pl.ds(64 * i, 64), pl.ds(C, C)] = both[:64]
        feats[pl.ds(64 * i, 64), pl.ds(2 * C, C)] = both[64:]

    for j in range(4):
        cols = pl.ds(256 * j, 256)
        bottle_pre[...] = dot(feats[...], stacked[:, cols])

        @pl.loop(0, 8)
        def _(r):
            rows = pl.ds(pl.multiple_of(64 * r, 64), 64)
            v = bottle_pre[rows, :]
            t = tanh_of(v)
            bottle[rows, cols] = (0.5 * v * (1.0 + t)).astype(BF16)
            bpg[rows, cols] = (bottle_grad[rows, cols].astype(F32) * gelu_slope(v, t)).astype(BF16)

    feats_grad = dot(bpg[...], stacked[...], 1, 1)
    direct[...] = feats_grad[:, :C]
    pair_grad = (SCALE * feats_grad[:, C:]).astype(BF16)
    for i in range(8):
        rows = pair_grad[64 * i : 64 * (i + 1)]
        stacked_rows = jnp.concatenate([rows[:, :C], rows[:, C:]], 0)
        filter2[0][:, i] = dot(z_tab[...], stacked_rows).astype(BF16).reshape(KZ, 16, C)

    def weight_sums():
        for j in range(GRP):
            cols = pl.ds(C * j, C)
            outer = dot(feats[...], bpg[:, cols], 0, 0).astype(BF16)
            for k in range(3):
                rows = outer[C * k : C * (k + 1)]
                sums_in[block_at(8 * k + j)] = rows.reshape(8, 16, C)
            rows = dot(bottle[:, cols], proj_grad[...], 0, 0).astype(BF16)
            sums_in[block_at(24 + j)] = rows.reshape(8, 16, C)
        first_sums.run(0)

    def write_cells():
        direct_out = dot(bottle[...], proj[...])
        for i in range(8):
            cell_grad[i] = direct_out[64 * i : 64 * (i + 1)]

        @pl.loop(0, 8)
        def _(i):
            spread = unpool(cell_grad[i], tmp)
            for half in range(2):
                x = 2 * i + half
                value = (hidden[x].astype(F32) + spread).reshape(16, 16, C)
                out[x] = (value * sea[x].astype(F32)).astype(BF16)

    x_filter(
        y_tab,
        x_tab,
        filter2,
        (weight_sums, lambda: first_sums.run(1), write_cells, lambda: first_sums.run(2)),
    )

    for i in range(8):
        modes = filter2[3][:, i].reshape(128, C)
        rows = dot(z_twice[...], modes, 0, 0)[:64] + direct[pl.ds(64 * i, 64), :]
        cell_grad[i] = 0.125 * rows
    acc[...] = jnp.zeros_like(acc)

    def tap_grads(i):
        spread = unpool(cell_grad[i], tmp)
        total = None
        for half in range(2):
            x = 2 * i + half
            upstream = (cot[x].astype(F32) * sea[x].astype(F32)).reshape(256, C) + spread
            value = pre[x]
            grad = (upstream * gelu_slope(value, tanh_of(value))).astype(BF16).astype(F32)
            shifted = jnp.concatenate(
                [shift_rows(grad, False), grad, shift_rows(grad, True)], 1
            ).astype(BF16)
            windows = rim_t[pl.ds(x, 3)].reshape(9 * C, 256)
            product = dot(windows, shifted)
            total = product if total is None else total + product
        acc[...] += total

    pl.loop(0, 4)(tap_grads)
    first_sums.run(3)
    pl.loop(4, 8)(tap_grads)

    for c in range(3):
        for ab in range(9):
            n = 9 * c + ab
            rows = acc[pl.ds(C * ab, C), pl.ds(C * c, C)].astype(BF16)
            taps_in[block_at(n)] = rows.reshape(8, 16, C)
    for n in range(27, 32):
        taps_in[block_at(n)] = jnp.zeros((8, 16, C), BF16)
    last_sums.run(0)
    first_sums.run(4)
    last_sums.run(1)
    first_sums.run(5)
    last_sums.run(2)
    first_sums.run(6)
    last_sums.run(3)

    total = jnp.zeros((C, C), F32)
    for p in range(2):
        for j in range(GRP):
            cols = pl.ds(C * j, C)
            grads = sums[block_at(8 * (1 + p) + j)].reshape(C, C)
            total += dot(grads, mix[p, :, cols], 1, 1)
    lift_mine[...] = total.astype(BF16)
    lift_copies = spread_rows(lift_mine, lift_parts, sem_lift, "grp")
    last_sums.run(4)
    arrived(lift_copies)
    left(lift_copies)
    last_sums.run(5)
    last_sums.run(6)
    left(halos)


def finish_kernel(out_in, sums, taps, lift_parts, lift_own, out, conv, lift, mix, proj, sem):
    copy = pltpu.make_async_copy(out_in, out, sem)
    copy.start()
    for c in range(3):
        for ab in range(9):
            conv[3 * ab + c] = taps[9 * c + ab].astype(F32)
    for j in range(GRP):
        cols = pl.ds(C * j, C)
        lift[:, cols] = sums[j].astype(F32) + lift_parts[j].astype(F32)
        proj[j] = sums[24 + j].astype(F32)
        for p in range(2):
            mix[p, :, cols] = dot(lift_own[...], sums[8 * (1 + p) + j], 0, 0)
    copy.wait()


def shards(
    field,
    sea,
    conv_weight,
    lift_weight,
    mix_weight,
    proj_weight,
    kx_modes,
    ky_modes,
    kz_modes,
    cotangent,
):
    sea_cells = jnp.broadcast_to(sea.astype(BF16)[..., None], field.shape)
    vmem = pl.BlockSpec(memory_space=pltpu.VMEM)
    smem = pl.BlockSpec(memory_space=pltpu.SMEM)
    hbm = pl.BlockSpec(memory_space=pl.ANY)
    out, sums, taps, lift_parts = pl.pallas_call(
        step_kernel,
        out_shape=(
            jax.ShapeDtypeStruct(field.shape, BF16),
            jax.ShapeDtypeStruct((2, 2, 4, 16, 16, C), BF16),
            jax.ShapeDtypeStruct((2, 2, 4, 16, 16, C), BF16),
            jax.ShapeDtypeStruct((GRP, C, C), BF16),
        ),
        in_specs=[hbm] * 7 + [smem] * 3,
        out_specs=(vmem,) * 4,
        scratch_shapes=[
            held(16, 16, 16, C),
            held(16, 16, 16, C),
            held(16, 16, 16, C),
            held(3, 3, 3, C, C),
            held(C, W),
            held(2, C, W),
            held(W, C),
            pltpu.SemaphoreType.DMA((7,)),
            held(64, 256),
            held(32, 128),
            held(64, 128),
            held(64, 64),
            held(128, 128),
            held(18, 18, 16, C),
            held(18, 3 * C, 256),
            held(2, 16, 16, C),
            held(2, 16, 16, C),
            held(4, 16, C),
            held(9 * C, 3 * C),
            held(16, 256, C, dtype=F32),
            held(16, 256, C),
            held(512, 3 * C),
            held(512, C),
            held(C, C),
            held(GRP, C, C),
            held(GRP, C, C),
            held(C, C),
            held(2, GRP, C, C),
            held(3 * C, W),
            held(512, 256, dtype=F32),
            held(512, W),
            held(512, W),
            held(512, W),
            held(512, C, dtype=F32),
            held(8, 64, C, dtype=F32),
            held(9 * C, 3 * C, dtype=F32),
            held(2, 2, 4, 16, 16, C),
            held(2, 2, 4, 16, 16, C),
            held(C, C),
            held(128, C, dtype=F32),
            pair_sems(8),
            pair_sems(GRP),
            pair_sems(GRP),
            pair_sems(1),
            pair_sems(GRP),
        ]
        + FILTER_SCRATCH()
        + FILTER_SCRATCH()
        + SUM_SCRATCH()
        + SUM_SCRATCH(),
        compiler_params=pltpu.CompilerParams(
            collective_id=1, has_side_effects=True, vmem_limit_bytes=56 * 2**20
        ),
        name="step",
    )(
        field,
        sea_cells,
        cotangent,
        conv_weight,
        lift_weight,
        mix_weight,
        proj_weight,
        kx_modes,
        ky_modes,
        kz_modes,
    )
    lift_own = lax.dynamic_slice_in_dim(lift_weight, lax.axis_index("grp") * C, C, 1)
    out, conv, lift, mix, proj = pl.pallas_call(
        finish_kernel,
        out_shape=(
            jax.ShapeDtypeStruct(field.shape, BF16),
            jax.ShapeDtypeStruct((27, C, C), F32),
            jax.ShapeDtypeStruct((C, W), F32),
            jax.ShapeDtypeStruct((2, C, W), F32),
            jax.ShapeDtypeStruct((GRP, C, C), F32),
        ),
        in_specs=[hbm] + [vmem] * 4,
        out_specs=(hbm,) + (vmem,) * 4,
        scratch_shapes=[pltpu.SemaphoreType.DMA(())],
        compiler_params=pltpu.CompilerParams(vmem_limit_bytes=32 * 2**20),
        name="finish",
    )(out, sums.reshape(32, C, C), taps.reshape(32, C, C), lift_parts, lift_own)
    return (out, conv.reshape(3, 3, 3, C, C), lift, mix, proj.reshape(W, C))


def solution(mesh):
    return jax.shard_map(
        shards,
        mesh=mesh,
        in_specs=(
            P("tile", "grp", None, None),
            P("tile", "grp", None),
            P(),
            P(),
            P(None, "grp", None),
            P(),
            P(),
            P(),
            P(),
            P("tile", "grp", None, None),
        ),
        out_specs=(P("tile", "grp", None, None), P(), P(), P(None, "grp", None), P()),
        check_vma=False,
    )
```

```python
import math

import jax
import jax.numpy as jnp
from jax import lax
from jax.experimental import pallas as pl
from jax.experimental.pallas import tpu as pltpu
from jax.sharding import PartitionSpec as P

BX = 128
BY = 64
BZ = 8
KX = 32
KY = 32
KZ = 4
C = 128
W = 1024
GRP = 8
TILE = 16
PAIRS = 8
SCALE = 1.0 / math.sqrt(BX * BY * BZ * KX * KY * KZ)
ROOT = math.sqrt(2.0 / math.pi)
CUBE = 0.044715
F32 = jnp.float32
BF16 = jnp.bfloat16
MESH = pl.DeviceIdType.MESH


def dot(first, second, left=1, right=0):
    return lax.dot_general(
        first, second, (((left,), (right,)), ((), ())), preferred_element_type=F32
    )


def grid_of(shape, dim):
    return lax.broadcasted_iota(jnp.int32, shape, dim)


def cos_sin(turns, length):
    angles = (turns & (length - 1)).astype(F32) * (2.0 * math.pi / length)
    return jnp.cos(angles), jnp.sin(angles)


def z_table(kz):
    shape = (64, 128)
    row, lane = grid_of(shape, 0), grid_of(shape, 1)
    freq = jnp.concatenate([jnp.full((16, 128), kz[b], jnp.int32) for b in range(KZ)], 0)
    cosine, sine = cos_sin(freq * (lane & 7), BZ)
    p, s = (row >> 3) & 1, lane >> 6
    value = jnp.where(s == p, jnp.where(s == 0, cosine, -cosine), -sine)
    return jnp.where((row & 7) == ((lane >> 3) & 7), value, 0.0)


def y_table(ky, first):
    shape = (32, 128)
    row, lane = grid_of(shape, 0), grid_of(shape, 1)
    freq = jnp.zeros(shape, jnp.int32)
    for a in range(16):
        freq = jnp.where((row >> 1) == a, ky[first + a], freq)
    y = ((lane >> 4) << 3) + (lane & 7)
    cosine, sine = cos_sin(freq * y, BY)
    p, q = (lane >> 3) & 1, row & 1
    return jnp.where(p == q, cosine, jnp.where(q == 0, sine, -sine))


def x_table(kx):
    shape = (32, 256)
    row, lane = grid_of(shape, 0), grid_of(shape, 1)
    freq = jnp.zeros(shape, jnp.int32)
    for k in range(KX):
        freq = jnp.where(row == k, kx[k], freq)
    x = ((lane >> 4) << 3) + (lane & 7)
    cosine, sine = cos_sin(freq * x, BX)
    even = ((lane >> 3) & 1) == 0
    return jnp.concatenate(
        [jnp.where(even, cosine, sine), jnp.where(even, -sine, cosine)], 0
    )


def spot(axis):
    return lax.axis_index(axis)


def place():
    grp, tile = spot("grp"), spot("tile")
    return {
        "xlo": grp // 4,
        "y": lax.rem(grp, 4),
        "z": tile // 4,
        "xhi": lax.rem(tile // 2, 2),
        "core": lax.rem(tile, 2),
    }


LENGTHS = {"xlo": 2, "y": 4, "z": 4, "xhi": 2, "core": 2}
DIGITS = {
    "grp": ("xlo", "y"),
    "tile": ("z", "xhi", "core"),
    "ring_y": ("y",),
    "ring_z": ("z",),
    "xz": ("xlo", "z", "xhi"),
    "xy": ("xlo", "y", "xhi"),
}
HOPS = {"xlo": (0, 1), "y": (0, 1, 2, 1), "z": (0, 1, 2, 1), "xhi": (0, 2), "core": (0, 0)}


def digits_of(name, number):
    digits = {}
    for part in reversed(DIGITS[name]):
        digits[part] = number % LENGTHS[part]
        number //= LENGTHS[part]
    return digits


def size_of(name):
    return math.prod(LENGTHS[part] for part in DIGITS[name])


def own(name):
    here = place()
    index = 0
    for part in DIGITS[name]:
        index = index * LENGTHS[part] + here[part]
    return index


def group(name):
    def hops(away):
        return sum(HOPS[part][step] for part, step in digits_of(name, away).items())

    for away in sorted(range(1, size_of(name)), key=lambda away: (-hops(away), away)):
        there = place()
        index = 0
        for part, step in digits_of(name, away).items():
            if step:
                there[part] = lax.rem(there[part] + step, LENGTHS[part])
        for part in DIGITS[name]:
            index = index * LENGTHS[part] + there[part]
        device = {
            "grp": there["xlo"] * 4 + there["y"],
            "tile": there["z"] * 4 + there["xhi"] * 2 + there["core"],
        }
        yield away, index, device


def partner():
    tile = spot("tile")
    return {"tile": tile + 1 - 2 * lax.rem(tile, 2)}


def near(step_tile, step_grp):
    target = {}
    if step_tile:
        target["tile"] = lax.rem(spot("tile") + step_tile + TILE, TILE)
    if step_grp:
        target["grp"] = lax.rem(spot("grp") + step_grp + GRP, GRP)
    return target


DIAGONALS = ((1, 1), (1, -1), (-1, 1), (-1, -1))


def greet():
    barrier = pltpu.get_barrier_semaphore()
    targets = [device for name in ("grp", "tile") for _, _, device in group(name)]
    targets += [near(*step) for step in DIAGONALS]
    for away, _, device in group("xz"):
        steps = digits_of("xz", away)
        if steps["xlo"] and (steps["z"] or steps["xhi"]):
            targets.append(device)
    for away, _, device in group("xy"):
        steps = digits_of("xy", away)
        if steps["xhi"] and steps["y"]:
            targets.append(device)
    for device in targets:
        pl.semaphore_signal(barrier, inc=1, device_id=device, device_id_type=MESH)
    return lambda: pl.semaphore_wait(barrier, len(targets))


def remote(src, dst, sems, place, device):
    copy = pltpu.make_async_remote_copy(
        src_ref=src,
        dst_ref=dst,
        send_sem=sems.at[0, place],
        recv_sem=sems.at[1, place],
        device_id=device,
        device_id_type=MESH,
    )
    copy.start()
    return copy


def scatter_rows(src, slots, sems, name):
    return [
        (away, remote(src.at[index], slots.at[away], sems, away, device))
        for away, index, device in group(name)
    ]


def add_rows(src, slots, copies, name):
    total = src[own(name)].astype(F32)
    for away, copy in reversed(copies):
        copy.wait_recv()
        total += slots[away].astype(F32)
    return total.astype(BF16)


def exchange(src, dst, sems, name):
    me = own(name)
    copies = [
        remote(src.at[index], dst.at[me], sems, away, device) for away, index, device in group(name)
    ]
    dst[me] = src[me]
    return copies


def spread_rows(src, dst, sems, name):
    me = own(name)
    copies = [remote(src, dst.at[me], sems, away, device) for away, index, device in group(name)]
    dst[me] = src[...]
    return copies


def arrived(copies):
    for copy in copies:
        copy.wait_recv()


def left(copies):
    for copy in copies:
        copy = copy[1] if isinstance(copy, tuple) else copy
        copy.wait_send()


def pair_sems(count):
    return pltpu.SemaphoreType.DMA((2, count))


def held(*shape, dtype=BF16):
    return pltpu.VMEM(shape, dtype)


FILTER_SCRATCH = (
    lambda: [held(KZ, 8, 16, C)]
    + [held(GRP, 8, 16, C) for _ in range(3)]
    + [held(TILE, 16, C) for _ in range(4)]
    + [held(256, C, dtype=F32)]
    + [pair_sems(GRP), pair_sems(TILE), pair_sems(TILE), pair_sems(GRP)]
)


def x_filter(y_tab, x_tab, work, beside):
    part, got_y, sent, back, mid, got, turned, home, wide, sem1, sem2, sem3, sem4 = work
    me = spot("grp")
    first = [
        remote(part.at[index // 2], got_y.at[me], sem1, away, device)
        for away, index, device in group("grp")
    ]
    got_y[me] = part[me // 2]
    beside[0]()
    arrived(first)
    for x in range(8):
        rows = got_y[:, x].reshape(128, C)
        wide[pl.ds(x, 32, stride=8), :] = dot(y_tab[...], rows)
    mid[...] = wide[...].astype(BF16).reshape(mid.shape)
    second = exchange(mid, got, sem2, "tile")
    beside[1]()
    arrived(second)
    modes = dot(x_tab[...], got[...].reshape(TILE * 16, C)).astype(BF16)
    turned[...] = dot(x_tab[...], modes, 0, 0).astype(BF16).reshape(turned.shape)
    third = exchange(turned, home, sem3, "tile")
    beside[2]()
    arrived(third)
    wide[...] = home[...].reshape(256, C).astype(F32)
    for x in range(8):
        rows = wide[pl.ds(x, 32, stride=8), :].astype(BF16)
        sent[:, x] = dot(y_tab[...], rows, 0, 0).astype(BF16).reshape(GRP, 16, C)
    fourth = exchange(sent, back, sem4, "grp")
    beside[3]()
    arrived(fourth)
    for copies in (first, second, third, fourth):
        left(copies)


SUM_SCRATCH = (
    lambda: [held(2, 4, 16, 16, C) for _ in range(2)]
    + [held(4, 16, 16, C) for _ in range(2)]
    + [held(16, 16, C) for _ in range(4)]
    + [held(16, C) for _ in range(2)]
    + [held(16, 16, C) for _ in range(2)]
    + [pair_sems(16) for _ in range(10)]
)


class Sums:
    def __init__(self, x, y, last, work):
        self.x, self.y, self.last = x, y, last
        self.buffers, self.sems = work[:12], work[12:]
        self.sent = []

    def run(self, step):
        x, y, s = self.x, self.y, self.sems
        got, mine, sa, sb, ma, mb, ra, rb, ta, tb, ga, gb = self.buffers
        core = place()["core"]
        if step == 0:
            self.a = [remote(x.at[1 - core], got, s[0], 0, partner())]
            self.b = []
        if step == 1:
            arrived(self.a)
            mine[...] = (x[core].astype(F32) + got[...].astype(F32)).astype(BF16)
            self.a = scatter_rows(mine.at[0], sa, s[1], "ring_y")
            self.b = scatter_rows(mine.at[1], sb, s[2], "ring_z")
        if step == 2:
            ma[...] = add_rows(mine.at[0], sa, self.a, "ring_y")
            self.a = scatter_rows(ma, ra, s[3], "xz")
            mb[...] = add_rows(mine.at[1], sb, self.b, "ring_z")
            self.b = scatter_rows(mb, rb, s[4], "xy")
        if step == 3:
            ta[...] = add_rows(ma, ra, self.a, "xz")
            self.a = spread_rows(ta, ga, s[5], "xz")
            tb[...] = add_rows(mb, rb, self.b, "xy")
            self.b = spread_rows(tb, gb, s[6], "xy")
        if step == 4:
            arrived(self.a)
            self.a = spread_rows(ga, y.at[core, 0], s[7], "ring_y")
            arrived(self.b)
            self.b = spread_rows(gb, y.at[core, 1], s[8], "ring_z")
        if step == 5:
            arrived(self.a)
            arrived(self.b)
            self.a = [remote(y.at[core], self.last.at[core], s[9], 0, partner())]
            self.b = []
        if step == 6:
            arrived(self.a)
            for copies in self.sent:
                left(copies)
            return
        self.sent += [self.a, self.b]


def block_at(n):
    return n // 16, n // 8 % 2, n % 8 // 2, pl.ds(8 * (n % 2), 8)


def tanh_of(x):
    return jnp.tanh(ROOT * (x + CUBE * x * x * x))


def gelu_slope(x, t):
    return 0.5 * (1.0 + t) + 0.5 * x * (1.0 - t * t) * (ROOT * (1.0 + 3.0 * CUBE * x * x))


def shift_rows(rows, forward):
    z = lax.rem(lax.broadcasted_iota(jnp.int32, rows.shape, 0), 16)
    if forward:
        return jnp.where(z == 0, 0.0, pltpu.roll(rows, 1, 0))
    return jnp.where(z == 15, 0.0, pltpu.roll(rows, rows.shape[0] - 1, 0))


def pool(rows, tmp):
    tmp[...] = rows.reshape(8, 2, 16, C).sum(1).reshape(128, C)
    return tmp[pl.ds(0, 64, stride=2), :] + tmp[pl.ds(1, 64, stride=2), :]


def unpool(rows, tmp):
    tmp[pl.ds(0, 64, stride=2), :] = rows
    tmp[pl.ds(1, 64, stride=2), :] = rows
    wide = jnp.broadcast_to(tmp[...].reshape(8, 1, 16, C), (8, 2, 16, C))
    return wide.reshape(256, C)


def step_kernel(
    field_in,
    sea_in,
    cot_in,
    conv_in,
    lift_in,
    mix_in,
    proj_in,
    kx,
    ky,
    kz,
    out_to,
    sums_to,
    taps_to,
    lift_to,
    field,
    sea_wide,
    sea,
    cot,
    conv_w,
    lift,
    mix,
    proj,
    load_sems,
    x_tab,
    y_tab,
    z_tab,
    z_cells,
    z_twice,
    rim,
    upstream,
    halo_x,
    halo_y,
    halo_c,
    conv_flat,
    pre,
    base,
    hidden,
    feats,
    proj_grad,
    lift_own,
    lm_part,
    lm_slots,
    lm_mine,
    lm_all,
    stacked,
    bottle_pre,
    bottle_grad,
    bottle,
    bpg,
    direct,
    cell_grad,
    acc,
    sums_in,
    taps_in,
    lift_mine,
    tmp,
    out,
    sums,
    taps,
    lift_parts,
    store_sems,
    sem_halo,
    sem_lm1,
    sem_lm2,
    sem_lm3,
    sem_lift,
    *work,
):
    count = len(FILTER_SCRATCH())
    filter1, filter2 = work[:count], work[count : 2 * count]
    work = work[2 * count :]
    count = len(SUM_SCRATCH())
    first_sums = Sums(sums_in, sums, sums, work[:count])
    last_sums = Sums(taps_in, taps, taps_to, work[count:])
    grp, tile = spot("grp"), spot("tile")
    core = place()["core"]

    def sea_of(x):
        return sea[pl.ds(pl.multiple_of(256 * x, 256), 256), :].reshape(16, 16, C)

    loads = []
    for i, (src, dst) in enumerate(
        (
            (field_in, field),
            (sea_in, sea_wide),
            (conv_in, conv_w),
            (lift_in, lift),
            (mix_in, mix),
            (cot_in, cot),
            (proj_in, proj),
        )
    ):
        loads.append(pltpu.make_async_copy(src, dst, load_sems.at[i]))
        loads[i].start()
    stores = [
        pltpu.make_async_copy(src, dst, store_sems.at[i])
        for i, (src, dst) in enumerate(
            ((out, out_to), (sums, sums_to), (lift_parts, lift_to), (taps.at[core], taps_to.at[core]))
        )
    ]
    met = greet()
    x_tab[...] = x_table(kx).astype(BF16)
    y_tab[...] = y_table(ky, 16 * lax.rem(grp, 2)).astype(BF16)
    z_values = z_table(kz).astype(BF16)
    z_tab[...] = z_values
    z_cells[...] = z_values[:, :64]
    for j in range(GRP):
        z_twice[pl.ds(16 * j, 16), :] = z_values[16 * (j // 2) : 16 * (j // 2 + 1)]
    loads[1].wait()
    lines = sea_wide[...].reshape(256, 16).astype(F32).astype(BF16)
    for z in range(16):
        pick = (grid_of((16, C), 0) == z).astype(F32).astype(BF16)
        sea[pl.ds(z, 256, stride=16), :] = dot(lines, pick)
    loads[0].wait()

    @pl.loop(0, 16)
    def _(x):
        rim[x + 1, 1:17] = (field[x].astype(F32) * sea_of(x)).astype(BF16)

    met()

    inner = pl.ds(1, 16)
    halos = [
        remote(rim.at[16, inner], halo_x.at[0], sem_halo, 0, near(1, 0)),
        remote(rim.at[1, inner], halo_x.at[1], sem_halo, 1, near(-1, 0)),
        remote(rim.at[inner, 16], halo_y.at[0], sem_halo, 2, near(0, 1)),
        remote(rim.at[inner, 1], halo_y.at[1], sem_halo, 3, near(0, -1)),
        remote(rim.at[16, 16], halo_c.at[0], sem_halo, 4, near(1, 1)),
        remote(rim.at[16, 1], halo_c.at[1], sem_halo, 5, near(1, -1)),
        remote(rim.at[1, 16], halo_c.at[2], sem_halo, 6, near(-1, 1)),
        remote(rim.at[1, 1], halo_c.at[3], sem_halo, 7, near(-1, -1)),
    ]
    for copy in loads[2:]:
        copy.wait()
    lift_own[...] = lift[:, pl.ds(pl.multiple_of(grp * C, C), C)]
    product = dot(lift_own[...], mix[core]).astype(BF16)
    for j in range(GRP):
        lm_part[j] = product[:, C * j : C * (j + 1)]

    for a in range(3):
        for b in range(3):
            for c in range(3):
                conv_flat[pl.ds(C * (3 * a + b), C), pl.ds(C * c, C)] = conv_w[a, b, c]

    @pl.loop(0, 8)
    def _(i):
        total = cot[2 * i].astype(F32) * sea_of(2 * i)
        total += cot[2 * i + 1].astype(F32) * sea_of(2 * i + 1)
        rows = pool(total.reshape(256, C), tmp)
        proj_grad[pl.ds(pl.multiple_of(64 * i, 64), 64), :] = rows.astype(BF16)

    stacked[pl.ds(0, C), :] = lift[...]
    arrived(halos)
    lm_first = scatter_rows(lm_part, lm_slots, sem_lm1, "grp")
    sides = (tile > 0, tile < TILE - 1, grp > 0, grp < GRP - 1)

    def keep(flag, rows):
        return jnp.where(flag, rows, jnp.zeros_like(rows))

    for side, x in ((0, 0), (1, 17)):
        rim[x, 1:17] = keep(sides[side], halo_x[side])
    for side, y in ((0, 0), (1, 17)):
        rim[1:17, y] = keep(sides[2 + side], halo_y[side])
    for i, x, y in ((0, 0, 0), (1, 0, 17), (2, 17, 0), (3, 17, 17)):
        flag = jnp.logical_and(sides[0 if x == 0 else 1], sides[2 if y == 0 else 3])
        rim[x, y] = keep(flag, halo_c[i])

    def windows():
        return jnp.concatenate(
            [rim[pl.ds(a, 16), b : b + 16].reshape(4096, C) for a in range(3) for b in range(3)], 1
        )

    product = dot(windows(), conv_flat[...])
    rows = (
        product[:, C : 2 * C]
        + shift_rows(product[:, :C], True)
        + shift_rows(product[:, 2 * C :], False)
    )
    pre[...] = rows.reshape(16, 256, C)
    hidden[...] = (0.5 * rows * (1.0 + tanh_of(rows))).astype(BF16).reshape(16, 256, C)

    for i in range(8):
        total = hidden[2 * i].astype(F32) + hidden[2 * i + 1].astype(F32)
        coarse = (0.125 * pool(total, tmp)).astype(BF16)
        feats[pl.ds(64 * i, 64), pl.ds(0, C)] = coarse
        filter1[0][:, i] = dot(z_cells[...], coarse).astype(BF16).reshape(KZ, 16, C)

    def back_through():
        for j in range(4):
            cols = pl.ds(256 * j, 256)
            bottle_grad[:, cols] = dot(proj_grad[...], proj[cols, :], 1, 1).astype(BF16)

    lm = {}

    def gather_lm():
        lm_mine[...] = add_rows(lm_part, lm_slots, lm_first, "grp")
        lm["grp"] = spread_rows(lm_mine, lm_all.at[core], sem_lm2, "grp")
        back_through()

    def swap_lm():
        arrived(lm["grp"])
        lm["core"] = [remote(lm_all.at[core], lm_all.at[core], sem_lm3, 0, partner())]

    def slopes():
        @pl.loop(0, 16)
        def _(x):
            value = pre[x]
            slope = gelu_slope(value, tanh_of(value))
            pre[x] = slope
            base[x] = slope * (cot[x].astype(F32) * sea_of(x)).reshape(256, C)

    x_filter(y_tab, x_tab, filter1, (lambda: None, gather_lm, slopes, swap_lm))

    arrived(lm["core"])
    for p in range(2):
        for j in range(GRP):
            stacked[pl.ds(C * (p + 1), C), pl.ds(C * j, C)] = lm_all[p, j]
    for copies in (lm_first, lm["grp"], lm["core"]):
        left(copies)

    for i in range(8):
        modes = filter1[3][:, i].reshape(128, C)
        both = (SCALE * dot(z_twice[...], modes, 0, 0)).astype(BF16)
        feats[pl.ds(64 * i, 64), pl.ds(C, C)] = both[:64]
        feats[pl.ds(64 * i, 64), pl.ds(2 * C, C)] = both[64:]

    for j in range(4):
        cols = pl.ds(256 * j, 256)
        bottle_pre[...] = dot(feats[...], stacked[:, cols])

        @pl.loop(0, 8)
        def _(r):
            rows = pl.ds(pl.multiple_of(64 * r, 64), 64)
            v = bottle_pre[rows, :]
            t = tanh_of(v)
            bottle[rows, cols] = (0.5 * v * (1.0 + t)).astype(BF16)
            bpg[rows, cols] = (bottle_grad[rows, cols].astype(F32) * gelu_slope(v, t)).astype(BF16)

    feats_grad = dot(bpg[...], stacked[...], 1, 1)
    direct[...] = feats_grad[:, :C]
    pair_grad = (SCALE * feats_grad[:, C:]).astype(BF16)
    for i in range(8):
        rows = pair_grad[64 * i : 64 * (i + 1)]
        stacked_rows = jnp.concatenate([rows[:, :C], rows[:, C:]], 0)
        filter2[0][:, i] = dot(z_tab[...], stacked_rows).astype(BF16).reshape(KZ, 16, C)

    def weight_sums():
        for j in range(GRP):
            cols = pl.ds(C * j, C)
            outer = dot(feats[...], bpg[:, cols], 0, 0).astype(BF16)
            for k in range(3):
                rows = outer[C * k : C * (k + 1)]
                sums_in[block_at(8 * k + j)] = rows.reshape(8, 16, C)
            rows = dot(bottle[:, cols], proj_grad[...], 0, 0).astype(BF16)
            sums_in[block_at(24 + j)] = rows.reshape(8, 16, C)
        first_sums.run(0)

    def write_cells():
        direct_out = dot(bottle[...], proj[...])
        for i in range(8):
            cell_grad[i] = direct_out[64 * i : 64 * (i + 1)]

        @pl.loop(0, 8)
        def _(i):
            spread = unpool(cell_grad[i], tmp)
            for half in range(2):
                x = 2 * i + half
                value = (hidden[x].astype(F32) + spread).reshape(16, 16, C)
                out[x] = (value * sea_of(x)).astype(BF16)

        stores[0].start()

    x_filter(
        y_tab,
        x_tab,
        filter2,
        (weight_sums, lambda: first_sums.run(1), write_cells, lambda: first_sums.run(2)),
    )

    for i in range(8):
        modes = filter2[3][:, i].reshape(128, C)
        rows = dot(z_twice[...], modes, 0, 0)[:64] + direct[pl.ds(64 * i, 64), :]
        cell_grad[i] = 0.125 * rows

    first_sums.run(3)

    @pl.loop(0, 8)
    def _(i):
        spread = unpool(cell_grad[i], tmp)
        for half in range(2):
            x = 2 * i + half
            grad = (base[x] + spread * pre[x]).astype(BF16).astype(F32)
            shifted = jnp.concatenate(
                [shift_rows(grad, False), grad, shift_rows(grad, True)], 1
            ).astype(BF16)
            upstream[:, pl.ds(pl.multiple_of(256 * x, 256), 256)] = shifted.T

    acc[...] = dot(upstream[...], windows()).astype(BF16)
    for c in range(3):
        for ab in range(9):
            rows = acc[pl.ds(C * c, C), pl.ds(C * ab, C)]
            taps_in[block_at(9 * c + ab)] = rows.reshape(8, 16, C)
    for n in range(27, 32):
        taps_in[block_at(n)] = jnp.zeros((8, 16, C), BF16)
    last_sums.run(0)
    first_sums.run(4)
    last_sums.run(1)
    first_sums.run(5)
    last_sums.run(2)
    first_sums.run(6)
    stores[1].start()
    last_sums.run(3)

    total = jnp.zeros((C, C), F32)
    for p in range(2):
        for j in range(GRP):
            cols = pl.ds(C * j, C)
            grads = sums[block_at(8 * (1 + p) + j)].reshape(C, C)
            total += dot(grads, mix[p, :, cols], 1, 1)
    lift_mine[...] = total.astype(BF16)
    lift_copies = spread_rows(lift_mine, lift_parts, sem_lift, "grp")
    last_sums.run(4)
    arrived(lift_copies)
    stores[2].start()
    left(lift_copies)
    left(halos)
    last_sums.run(5)
    stores[3].start()
    last_sums.run(6)
    for copy in stores:
        copy.wait()


def finish_kernel(
    out_in,
    sums_in,
    taps_in,
    parts_in,
    lift_in,
    out_to,
    conv_to,
    lift_to,
    mix_to,
    proj_to,
    out,
    sums,
    taps,
    parts,
    own_rows,
    conv,
    lift,
    mix,
    proj,
    sems,
):
    def copies(first, *pairs):
        return [
            pltpu.make_async_copy(src, dst, sems.at[first + i])
            for i, (src, dst) in enumerate(pairs)
        ]

    cols = pl.ds(pl.multiple_of(spot("grp") * C, C), C)
    loads = copies(
        0,
        (taps_in, taps),
        (sums_in, sums),
        (parts_in, parts),
        (lift_in.at[:, cols], own_rows),
        (out_in, out),
    )
    stores = copies(5, (conv, conv_to), (lift, lift_to), (mix, mix_to), (proj, proj_to), (out, out_to))
    for copy in loads:
        copy.start()
    loads[0].wait()
    for c in range(3):
        for ab in range(9):
            conv[3 * ab + c] = taps[9 * c + ab].astype(F32).T
    stores[0].start()
    for copy in loads[1:4]:
        copy.wait()
    for j in range(GRP):
        cols = pl.ds(C * j, C)
        lift[:, cols] = sums[j].astype(F32) + parts[j].astype(F32)
        proj[j] = sums[24 + j].astype(F32)
        for p in range(2):
            mix[p, :, cols] = dot(own_rows[...], sums[8 * (1 + p) + j], 0, 0)
    for copy in stores[1:4]:
        copy.start()
    loads[4].wait()
    stores[4].start()
    for copy in stores:
        copy.wait()


def shards(
    field,
    sea,
    conv_weight,
    lift_weight,
    mix_weight,
    proj_weight,
    kx_modes,
    ky_modes,
    kz_modes,
    cotangent,
):
    smem = pl.BlockSpec(memory_space=pltpu.SMEM)
    hbm = pl.BlockSpec(memory_space=pl.ANY)
    out, sums, taps, lift_parts = pl.pallas_call(
        step_kernel,
        out_shape=(
            jax.ShapeDtypeStruct(field.shape, BF16),
            jax.ShapeDtypeStruct((2, 2, 4, 16, 16, C), BF16),
            jax.ShapeDtypeStruct((2, 2, 4, 16, 16, C), BF16),
            jax.ShapeDtypeStruct((GRP, C, C), BF16),
        ),
        in_specs=[hbm] * 7 + [smem] * 3,
        out_specs=(hbm,) * 4,
        scratch_shapes=[
            held(16, 16, 16, C),
            pltpu.VMEM((16, 16, 16), jnp.int32),
            held(4096, C, dtype=F32),
            held(16, 16, 16, C),
            held(3, 3, 3, C, C),
            held(C, W),
            held(2, C, W),
            held(W, C),
            pltpu.SemaphoreType.DMA((7,)),
            held(64, 256),
            held(32, 128),
            held(64, 128),
            held(64, 64),
            held(128, 128),
            held(18, 18, 16, C),
            held(3 * C, 4096),
            held(2, 16, 16, C),
            held(2, 16, 16, C),
            held(4, 16, C),
            held(9 * C, 3 * C),
            held(16, 256, C, dtype=F32),
            held(16, 256, C, dtype=F32),
            held(16, 256, C),
            held(512, 3 * C),
            held(512, C),
            held(C, C),
            held(GRP, C, C),
            held(GRP, C, C),
            held(C, C),
            held(2, GRP, C, C),
            held(3 * C, W),
            held(512, 256, dtype=F32),
            held(512, W),
            held(512, W),
            held(512, W),
            held(512, C, dtype=F32),
            held(8, 64, C, dtype=F32),
            held(3 * C, 9 * C),
            held(2, 2, 4, 16, 16, C),
            held(2, 2, 4, 16, 16, C),
            held(C, C),
            held(128, C, dtype=F32),
            held(16, 16, 16, C),
            held(2, 2, 4, 16, 16, C),
            held(2, 2, 4, 16, 16, C),
            held(GRP, C, C),
            pltpu.SemaphoreType.DMA((4,)),
            pair_sems(8),
            pair_sems(GRP),
            pair_sems(GRP),
            pair_sems(1),
            pair_sems(GRP),
        ]
        + FILTER_SCRATCH()
        + FILTER_SCRATCH()
        + SUM_SCRATCH()
        + SUM_SCRATCH(),
        compiler_params=pltpu.CompilerParams(
            collective_id=1, has_side_effects=True, vmem_limit_bytes=56 * 2**20
        ),
        name="step",
    )(
        field,
        sea,
        cotangent,
        conv_weight,
        lift_weight,
        mix_weight,
        proj_weight,
        kx_modes,
        ky_modes,
        kz_modes,
    )
    out, conv, lift, mix, proj = pl.pallas_call(
        finish_kernel,
        out_shape=(
            jax.ShapeDtypeStruct(field.shape, BF16),
            jax.ShapeDtypeStruct((27, C, C), F32),
            jax.ShapeDtypeStruct((C, W), F32),
            jax.ShapeDtypeStruct((2, C, W), F32),
            jax.ShapeDtypeStruct((GRP, C, C), F32),
        ),
        in_specs=[hbm] * 5,
        out_specs=(hbm,) * 5,
        scratch_shapes=[
            held(16, 16, 16, C),
            held(32, C, C),
            held(32, C, C),
            held(GRP, C, C),
            held(C, C),
            held(27, C, C, dtype=F32),
            held(C, W, dtype=F32),
            held(2, C, W, dtype=F32),
            held(GRP, C, C, dtype=F32),
            pltpu.SemaphoreType.DMA((10,)),
        ],
        compiler_params=pltpu.CompilerParams(vmem_limit_bytes=56 * 2**20),
        name="finish",
    )(out, sums.reshape(32, C, C), taps.reshape(32, C, C), lift_parts, lift_weight)
    return (out, conv.reshape(3, 3, 3, C, C), lift, mix, proj.reshape(W, C))


def solution(mesh):
    return jax.shard_map(
        shards,
        mesh=mesh,
        in_specs=(
            P("tile", "grp", None, None),
            P("tile", "grp", None),
            P(),
            P(),
            P(None, "grp", None),
            P(),
            P(),
            P(),
            P(),
            P("tile", "grp", None, None),
        ),
        out_specs=(P("tile", "grp", None, None), P(), P(), P(None, "grp", None), P()),
        check_vma=False,
    )
```

```python
import math

import jax
import jax.numpy as jnp
from jax import lax
from jax.experimental import pallas as pl
from jax.experimental.pallas import tpu as pltpu
from jax.sharding import PartitionSpec as P

BX = 128
BY = 64
BZ = 8
KX = 32
KY = 32
KZ = 4
C = 128
W = 1024
GRP = 8
TILE = 16
PAIRS = 8
SCALE = 1.0 / math.sqrt(BX * BY * BZ * KX * KY * KZ)
ROOT = math.sqrt(2.0 / math.pi)
CUBE = 0.044715
F32 = jnp.float32
BF16 = jnp.bfloat16
MESH = pl.DeviceIdType.MESH


def dot(first, second, left=1, right=0):
    return lax.dot_general(
        first, second, (((left,), (right,)), ((), ())), preferred_element_type=F32
    )


def grid_of(shape, dim):
    return lax.broadcasted_iota(jnp.int32, shape, dim)


def cos_sin(turns, length):
    angles = (turns & (length - 1)).astype(F32) * (2.0 * math.pi / length)
    return jnp.cos(angles), jnp.sin(angles)


def z_table(kz):
    shape = (64, 128)
    row, lane = grid_of(shape, 0), grid_of(shape, 1)
    freq = jnp.concatenate([jnp.full((16, 128), kz[b], jnp.int32) for b in range(KZ)], 0)
    cosine, sine = cos_sin(freq * (lane & 7), BZ)
    p, s = (row >> 3) & 1, lane >> 6
    value = jnp.where(s == p, jnp.where(s == 0, cosine, -cosine), -sine)
    return jnp.where((row & 7) == ((lane >> 3) & 7), value, 0.0)


def y_table(ky, first):
    shape = (32, 128)
    row, lane = grid_of(shape, 0), grid_of(shape, 1)
    freq = jnp.zeros(shape, jnp.int32)
    for a in range(16):
        freq = jnp.where((row >> 1) == a, ky[first + a], freq)
    y = ((lane >> 4) << 3) + (lane & 7)
    cosine, sine = cos_sin(freq * y, BY)
    p, q = (lane >> 3) & 1, row & 1
    return jnp.where(p == q, cosine, jnp.where(q == 0, sine, -sine))


def x_table(kx):
    shape = (32, 256)
    row, lane = grid_of(shape, 0), grid_of(shape, 1)
    freq = jnp.zeros(shape, jnp.int32)
    for k in range(KX):
        freq = jnp.where(row == k, kx[k], freq)
    x = ((lane >> 4) << 3) + (lane & 7)
    cosine, sine = cos_sin(freq * x, BX)
    even = ((lane >> 3) & 1) == 0
    return jnp.concatenate(
        [jnp.where(even, cosine, sine), jnp.where(even, -sine, cosine)], 0
    )


def spot(axis):
    return lax.axis_index(axis)


def place():
    grp, tile = spot("grp"), spot("tile")
    return {
        "xlo": grp // 4,
        "y": lax.rem(grp, 4),
        "z": tile // 4,
        "xhi": lax.rem(tile // 2, 2),
        "core": lax.rem(tile, 2),
    }


LENGTHS = {"xlo": 2, "y": 4, "z": 4, "xhi": 2, "core": 2}
DIGITS = {
    "grp": ("xlo", "y"),
    "tile": ("z", "xhi", "core"),
    "ring_y": ("y",),
    "ring_z": ("z",),
    "xz": ("xlo", "z", "xhi"),
    "xy": ("xlo", "y", "xhi"),
}
HOPS = {"xlo": (0, 1), "y": (0, 1, 2, 1), "z": (0, 1, 2, 1), "xhi": (0, 2), "core": (0, 0)}


def digits_of(name, number):
    digits = {}
    for part in reversed(DIGITS[name]):
        digits[part] = number % LENGTHS[part]
        number //= LENGTHS[part]
    return digits


def size_of(name):
    return math.prod(LENGTHS[part] for part in DIGITS[name])


def own(name):
    here = place()
    index = 0
    for part in DIGITS[name]:
        index = index * LENGTHS[part] + here[part]
    return index


def group(name):
    def hops(away):
        return sum(HOPS[part][step] for part, step in digits_of(name, away).items())

    for away in sorted(range(1, size_of(name)), key=lambda away: (-hops(away), away)):
        there = place()
        index = 0
        for part, step in digits_of(name, away).items():
            if step:
                there[part] = lax.rem(there[part] + step, LENGTHS[part])
        for part in DIGITS[name]:
            index = index * LENGTHS[part] + there[part]
        device = {
            "grp": there["xlo"] * 4 + there["y"],
            "tile": there["z"] * 4 + there["xhi"] * 2 + there["core"],
        }
        yield away, index, device


def partner():
    tile = spot("tile")
    return {"tile": tile + 1 - 2 * lax.rem(tile, 2)}


def near(step_tile, step_grp):
    target = {}
    if step_tile:
        target["tile"] = lax.rem(spot("tile") + step_tile + TILE, TILE)
    if step_grp:
        target["grp"] = lax.rem(spot("grp") + step_grp + GRP, GRP)
    return target


DIAGONALS = ((1, 1), (1, -1), (-1, 1), (-1, -1))


def greet():
    barrier = pltpu.get_barrier_semaphore()
    targets = [device for name in ("grp", "tile") for _, _, device in group(name)]
    targets += [near(*step) for step in DIAGONALS]
    for away, _, device in group("xz"):
        steps = digits_of("xz", away)
        if steps["xlo"] and (steps["z"] or steps["xhi"]):
            targets.append(device)
    for away, _, device in group("xy"):
        steps = digits_of("xy", away)
        if steps["xhi"] and steps["y"]:
            targets.append(device)
    for device in targets:
        pl.semaphore_signal(barrier, inc=1, device_id=device, device_id_type=MESH)
    return lambda: pl.semaphore_wait(barrier, len(targets))


def remote(src, dst, sems, device):
    pltpu.make_async_remote_copy(
        src_ref=src,
        dst_ref=dst,
        send_sem=sems.at[0],
        recv_sem=sems.at[1],
        device_id=device,
        device_id_type=MESH,
    ).start()


class Sent:
    def __init__(self, all, sems):
        self.all, self.sems = all, sems

    def wait_send(self):
        pltpu.make_async_copy(self.all, self.all, self.sems.at[0]).wait()

    def wait_recv(self):
        pltpu.make_async_copy(self.all, self.all, self.sems.at[1]).wait()


def to_partner(src, dst, sems):
    remote(src, dst, sems, partner())
    return Sent(dst, sems)


def scatter_rows(src, slots, sems, name):
    for away, index, device in group(name):
        remote(src.at[index], slots.at[away], sems, device)
    return Sent(slots.at[pl.ds(1, size_of(name) - 1)], sems)


def add_rows(src, slots, copies, name):
    copies.wait_recv()
    total = src[own(name)].astype(F32)
    for away in range(1, size_of(name)):
        total += slots[away].astype(F32)
    return total.astype(BF16)


def exchange(src, dst, sems, name, share=1):
    me = own(name)
    for away, index, device in group(name):
        remote(src.at[index // share], dst.at[me], sems, device)
    dst[me] = src[me // share]
    return Sent(dst.at[pl.ds(1, size_of(name) - 1)], sems)


def spread_rows(src, dst, sems, name):
    me = own(name)
    for away, index, device in group(name):
        remote(src, dst.at[me], sems, device)
    dst[me] = src[...]
    return Sent(dst.at[pl.ds(1, size_of(name) - 1)], sems)


def pair_sems():
    return pltpu.SemaphoreType.DMA((2,))


def held(*shape, dtype=BF16):
    return pltpu.VMEM(shape, dtype)


FILTER_SCRATCH = (
    lambda: [held(KZ, 8, 16, C)]
    + [held(GRP, 8, 16, C) for _ in range(3)]
    + [held(TILE, 16, C) for _ in range(4)]
    + [held(256, C, dtype=F32)]
    + [pair_sems() for _ in range(4)]
)


def x_filter(y_tab, x_tab, work, beside):
    part, got_y, sent, back, mid, got, turned, home, wide, sem1, sem2, sem3, sem4 = work
    first = exchange(part, got_y, sem1, "grp", 2)
    beside[0]()
    first.wait_recv()
    for x in range(8):
        rows = got_y[:, x].reshape(128, C)
        wide[pl.ds(x, 32, stride=8), :] = dot(y_tab[...], rows)
    mid[...] = wide[...].astype(BF16).reshape(mid.shape)
    second = exchange(mid, got, sem2, "tile")
    beside[1]()
    second.wait_recv()
    modes = dot(x_tab[...], got[...].reshape(TILE * 16, C)).astype(BF16)
    turned[...] = dot(x_tab[...], modes, 0, 0).astype(BF16).reshape(turned.shape)
    third = exchange(turned, home, sem3, "tile")
    beside[2]()
    third.wait_recv()
    wide[...] = home[...].reshape(256, C).astype(F32)
    for x in range(8):
        rows = wide[pl.ds(x, 32, stride=8), :].astype(BF16)
        sent[:, x] = dot(y_tab[...], rows, 0, 0).astype(BF16).reshape(GRP, 16, C)
    fourth = exchange(sent, back, sem4, "grp")
    beside[3]()
    fourth.wait_recv()
    for copies in (first, second, third, fourth):
        copies.wait_send()


SUM_SCRATCH = (
    lambda: [held(2, 4, 16, 16, C) for _ in range(2)]
    + [held(4, 16, 16, C) for _ in range(2)]
    + [held(16, 16, C) for _ in range(4)]
    + [held(16, C) for _ in range(2)]
    + [held(16, 16, C) for _ in range(2)]
    + [pair_sems() for _ in range(10)]
)


class Sums:
    def __init__(self, x, y, last, work):
        self.x, self.y, self.last = x, y, last
        self.buffers, self.sems = work[:12], work[12:]
        self.sent = []

    def run(self, step):
        x, y, s = self.x, self.y, self.sems
        got, mine, sa, sb, ma, mb, ra, rb, ta, tb, ga, gb = self.buffers
        core = place()["core"]
        if step == 0:
            self.a = to_partner(x.at[1 - core], got, s[0])
        if step == 1:
            self.a.wait_recv()
            mine[...] = (x[core].astype(F32) + got[...].astype(F32)).astype(BF16)
            self.a = scatter_rows(mine.at[0], sa, s[1], "ring_y")
            self.b = scatter_rows(mine.at[1], sb, s[2], "ring_z")
        if step == 2:
            ma[...] = add_rows(mine.at[0], sa, self.a, "ring_y")
            self.a = scatter_rows(ma, ra, s[3], "xz")
            mb[...] = add_rows(mine.at[1], sb, self.b, "ring_z")
            self.b = scatter_rows(mb, rb, s[4], "xy")
        if step == 3:
            ta[...] = add_rows(ma, ra, self.a, "xz")
            self.a = spread_rows(ta, ga, s[5], "xz")
            tb[...] = add_rows(mb, rb, self.b, "xy")
            self.b = spread_rows(tb, gb, s[6], "xy")
        if step == 4:
            self.a.wait_recv()
            self.a = spread_rows(ga, y.at[core, 0], s[7], "ring_y")
            self.b.wait_recv()
            self.b = spread_rows(gb, y.at[core, 1], s[8], "ring_z")
        if step == 5:
            self.a.wait_recv()
            self.b.wait_recv()
            self.a = to_partner(y.at[core], self.last.at[core], s[9])
        if step == 6:
            self.a.wait_recv()
            for copies in self.sent:
                copies.wait_send()
            return
        self.sent += [self.a] if step in (0, 5) else [self.a, self.b]


def block_at(n):
    return n // 16, n // 8 % 2, n % 8 // 2, pl.ds(8 * (n % 2), 8)


def tanh_of(x):
    return jnp.tanh(ROOT * (x + CUBE * x * x * x))


def gelu_slope(x, t):
    return 0.5 * (1.0 + t) + 0.5 * x * (1.0 - t * t) * (ROOT * (1.0 + 3.0 * CUBE * x * x))


def shift_rows(rows, forward):
    z = lax.rem(lax.broadcasted_iota(jnp.int32, rows.shape, 0), 16)
    if forward:
        return jnp.where(z == 0, 0.0, pltpu.roll(rows, 1, 0))
    return jnp.where(z == 15, 0.0, pltpu.roll(rows, rows.shape[0] - 1, 0))


def pool(rows, tmp):
    tmp[...] = rows.reshape(8, 2, 16, C).sum(1).reshape(128, C)
    return tmp[pl.ds(0, 64, stride=2), :] + tmp[pl.ds(1, 64, stride=2), :]


def unpool(rows, tmp):
    tmp[pl.ds(0, 64, stride=2), :] = rows
    tmp[pl.ds(1, 64, stride=2), :] = rows
    wide = jnp.broadcast_to(tmp[...].reshape(8, 1, 16, C), (8, 2, 16, C))
    return wide.reshape(256, C)


def step_kernel(
    field_in,
    sea_in,
    cot_in,
    conv_in,
    lift_in,
    mix_in,
    proj_in,
    kx,
    ky,
    kz,
    out_to,
    sums_to,
    taps_to,
    lift_to,
    field,
    sea_wide,
    sea,
    cot,
    conv_w,
    lift,
    mix,
    proj,
    load_sems,
    x_tab,
    y_tab,
    z_tab,
    z_cells,
    z_twice,
    rim,
    upstream,
    halo_x,
    halo_y,
    halo_c,
    conv_flat,
    pre,
    base,
    hidden,
    feats,
    proj_grad,
    lift_own,
    lm_part,
    lm_slots,
    lm_mine,
    lm_all,
    stacked,
    bottle_pre,
    bottle_grad,
    bottle,
    bpg,
    direct,
    cell_grad,
    acc,
    sums_in,
    taps_in,
    lift_mine,
    tmp,
    out,
    sums,
    taps,
    lift_parts,
    store_sems,
    sem_halo,
    sem_lm1,
    sem_lm2,
    sem_lm3,
    sem_lift,
    *work,
):
    count = len(FILTER_SCRATCH())
    filter1, filter2 = work[:count], work[count : 2 * count]
    work = work[2 * count :]
    count = len(SUM_SCRATCH())
    first_sums = Sums(sums_in, sums, sums, work[:count])
    last_sums = Sums(taps_in, taps, taps_to, work[count:])
    grp, tile = spot("grp"), spot("tile")
    core = place()["core"]

    def sea_of(x):
        return sea[pl.ds(pl.multiple_of(256 * x, 256), 256), :].reshape(16, 16, C)

    loads = []
    for i, (src, dst) in enumerate(
        (
            (field_in, field),
            (sea_in, sea_wide),
            (conv_in, conv_w),
            (lift_in, lift),
            (mix_in, mix),
            (cot_in, cot),
            (proj_in, proj),
        )
    ):
        loads.append(pltpu.make_async_copy(src, dst, load_sems.at[i]))
        loads[i].start()
    stores = [
        pltpu.make_async_copy(src, dst, store_sems.at[i])
        for i, (src, dst) in enumerate(
            ((out, out_to), (sums, sums_to), (lift_parts, lift_to), (taps.at[core], taps_to.at[core]))
        )
    ]
    met = greet()
    x_tab[...] = x_table(kx).astype(BF16)
    y_tab[...] = y_table(ky, 16 * lax.rem(grp, 2)).astype(BF16)
    z_values = z_table(kz).astype(BF16)
    z_tab[...] = z_values
    z_cells[...] = z_values[:, :64]
    for j in range(GRP):
        z_twice[pl.ds(16 * j, 16), :] = z_values[16 * (j // 2) : 16 * (j // 2 + 1)]
    loads[1].wait()
    lines = sea_wide[...].reshape(256, 16).astype(F32).astype(BF16)
    for z in range(16):
        pick = (grid_of((16, C), 0) == z).astype(F32).astype(BF16)
        sea[pl.ds(z, 256, stride=16), :] = dot(lines, pick)
    loads[0].wait()

    @pl.loop(0, 16)
    def _(x):
        rim[x + 1, 1:17] = (field[x].astype(F32) * sea_of(x)).astype(BF16)

    met()

    inner = pl.ds(1, 16)
    strip_x, strip_y, corner = sem_halo.at[0], sem_halo.at[1], sem_halo.at[2]
    remote(rim.at[16, 16], halo_c.at[0], corner, near(1, 1))
    remote(rim.at[16, 1], halo_c.at[1], corner, near(1, -1))
    remote(rim.at[1, 16], halo_c.at[2], corner, near(-1, 1))
    remote(rim.at[1, 1], halo_c.at[3], corner, near(-1, -1))
    remote(rim.at[16, inner], halo_x.at[0], strip_x, near(1, 0))
    remote(rim.at[1, inner], halo_x.at[1], strip_x, near(-1, 0))
    remote(rim.at[inner, 16], halo_y.at[0], strip_y, near(0, 1))
    remote(rim.at[inner, 1], halo_y.at[1], strip_y, near(0, -1))
    halos = (Sent(halo_c, corner), Sent(halo_x, strip_x), Sent(halo_y, strip_y))
    for copy in loads[2:]:
        copy.wait()
    lift_own[...] = lift[:, pl.ds(pl.multiple_of(grp * C, C), C)]
    product = dot(lift_own[...], mix[core]).astype(BF16)
    for j in range(GRP):
        lm_part[j] = product[:, C * j : C * (j + 1)]

    for a in range(3):
        for b in range(3):
            for c in range(3):
                conv_flat[pl.ds(C * (3 * a + b), C), pl.ds(C * c, C)] = conv_w[a, b, c]

    @pl.loop(0, 8)
    def _(i):
        total = cot[2 * i].astype(F32) * sea_of(2 * i)
        total += cot[2 * i + 1].astype(F32) * sea_of(2 * i + 1)
        rows = pool(total.reshape(256, C), tmp)
        proj_grad[pl.ds(pl.multiple_of(64 * i, 64), 64), :] = rows.astype(BF16)

    stacked[pl.ds(0, C), :] = lift[...]
    for copies in halos:
        copies.wait_recv()
    lm_first = scatter_rows(lm_part, lm_slots, sem_lm1, "grp")
    sides = (tile > 0, tile < TILE - 1, grp > 0, grp < GRP - 1)

    def keep(flag, rows):
        return jnp.where(flag, rows, jnp.zeros_like(rows))

    for side, x in ((0, 0), (1, 17)):
        rim[x, 1:17] = keep(sides[side], halo_x[side])
    for side, y in ((0, 0), (1, 17)):
        rim[1:17, y] = keep(sides[2 + side], halo_y[side])
    for i, x, y in ((0, 0, 0), (1, 0, 17), (2, 17, 0), (3, 17, 17)):
        flag = jnp.logical_and(sides[0 if x == 0 else 1], sides[2 if y == 0 else 3])
        rim[x, y] = keep(flag, halo_c[i])

    def windows():
        return jnp.concatenate(
            [rim[pl.ds(a, 16), b : b + 16].reshape(4096, C) for a in range(3) for b in range(3)], 1
        )

    product = dot(windows(), conv_flat[...])
    rows = (
        product[:, C : 2 * C]
        + shift_rows(product[:, :C], True)
        + shift_rows(product[:, 2 * C :], False)
    )
    pre[...] = rows.reshape(16, 256, C)
    hidden[...] = (0.5 * rows * (1.0 + tanh_of(rows))).astype(BF16).reshape(16, 256, C)

    for i in range(8):
        total = hidden[2 * i].astype(F32) + hidden[2 * i + 1].astype(F32)
        coarse = (0.125 * pool(total, tmp)).astype(BF16)
        feats[pl.ds(64 * i, 64), pl.ds(0, C)] = coarse
        filter1[0][:, i] = dot(z_cells[...], coarse).astype(BF16).reshape(KZ, 16, C)

    def back_through():
        for j in range(4):
            cols = pl.ds(256 * j, 256)
            bottle_grad[:, cols] = dot(proj_grad[...], proj[cols, :], 1, 1).astype(BF16)

    lm = {}

    def gather_lm():
        lm_mine[...] = add_rows(lm_part, lm_slots, lm_first, "grp")
        lm["grp"] = spread_rows(lm_mine, lm_all.at[core], sem_lm2, "grp")
        back_through()

    def swap_lm():
        lm["grp"].wait_recv()
        lm["core"] = to_partner(lm_all.at[core], lm_all.at[core], sem_lm3)

    def slopes():
        @pl.loop(0, 16)
        def _(x):
            value = pre[x]
            slope = gelu_slope(value, tanh_of(value))
            pre[x] = slope
            base[x] = slope * (cot[x].astype(F32) * sea_of(x)).reshape(256, C)

    x_filter(y_tab, x_tab, filter1, (lambda: None, gather_lm, slopes, swap_lm))

    lm["core"].wait_recv()
    for p in range(2):
        for j in range(GRP):
            stacked[pl.ds(C * (p + 1), C), pl.ds(C * j, C)] = lm_all[p, j]
    for copies in (lm_first, lm["grp"], lm["core"]):
        copies.wait_send()

    for i in range(8):
        modes = filter1[3][:, i].reshape(128, C)
        both = (SCALE * dot(z_twice[...], modes, 0, 0)).astype(BF16)
        feats[pl.ds(64 * i, 64), pl.ds(C, C)] = both[:64]
        feats[pl.ds(64 * i, 64), pl.ds(2 * C, C)] = both[64:]

    for j in range(4):
        cols = pl.ds(256 * j, 256)
        bottle_pre[...] = dot(feats[...], stacked[:, cols])

        @pl.loop(0, 8)
        def _(r):
            rows = pl.ds(pl.multiple_of(64 * r, 64), 64)
            v = bottle_pre[rows, :]
            t = tanh_of(v)
            bottle[rows, cols] = (0.5 * v * (1.0 + t)).astype(BF16)
            bpg[rows, cols] = (bottle_grad[rows, cols].astype(F32) * gelu_slope(v, t)).astype(BF16)

    feats_grad = dot(bpg[...], stacked[...], 1, 1)
    direct[...] = feats_grad[:, :C]
    pair_grad = (SCALE * feats_grad[:, C:]).astype(BF16)
    for i in range(8):
        rows = pair_grad[64 * i : 64 * (i + 1)]
        stacked_rows = jnp.concatenate([rows[:, :C], rows[:, C:]], 0)
        filter2[0][:, i] = dot(z_tab[...], stacked_rows).astype(BF16).reshape(KZ, 16, C)

    def weight_sums():
        for j in range(GRP):
            cols = pl.ds(C * j, C)
            outer = dot(feats[...], bpg[:, cols], 0, 0).astype(BF16)
            for k in range(3):
                rows = outer[C * k : C * (k + 1)]
                sums_in[block_at(8 * k + j)] = rows.reshape(8, 16, C)
            rows = dot(bottle[:, cols], proj_grad[...], 0, 0).astype(BF16)
            sums_in[block_at(24 + j)] = rows.reshape(8, 16, C)
        first_sums.run(0)

    def write_cells():
        direct_out = dot(bottle[...], proj[...])
        for i in range(8):
            cell_grad[i] = direct_out[64 * i : 64 * (i + 1)]

        @pl.loop(0, 8)
        def _(i):
            spread = unpool(cell_grad[i], tmp)
            for half in range(2):
                x = 2 * i + half
                value = (hidden[x].astype(F32) + spread).reshape(16, 16, C)
                out[x] = (value * sea_of(x)).astype(BF16)

        stores[0].start()

    x_filter(
        y_tab,
        x_tab,
        filter2,
        (weight_sums, lambda: first_sums.run(1), write_cells, lambda: first_sums.run(2)),
    )

    for i in range(8):
        modes = filter2[3][:, i].reshape(128, C)
        rows = dot(z_twice[...], modes, 0, 0)[:64] + direct[pl.ds(64 * i, 64), :]
        cell_grad[i] = 0.125 * rows

    first_sums.run(3)

    @pl.loop(0, 8)
    def _(i):
        spread = unpool(cell_grad[i], tmp)
        for half in range(2):
            x = 2 * i + half
            grad = (base[x] + spread * pre[x]).astype(BF16).astype(F32)
            shifted = jnp.concatenate(
                [shift_rows(grad, False), grad, shift_rows(grad, True)], 1
            ).astype(BF16)
            upstream[:, pl.ds(pl.multiple_of(256 * x, 256), 256)] = shifted.T

    acc[...] = dot(upstream[...], windows()).astype(BF16)
    for c in range(3):
        for ab in range(9):
            rows = acc[pl.ds(C * c, C), pl.ds(C * ab, C)]
            taps_in[block_at(9 * c + ab)] = rows.reshape(8, 16, C)
    for n in range(27, 32):
        taps_in[block_at(n)] = jnp.zeros((8, 16, C), BF16)
    last_sums.run(0)
    first_sums.run(4)
    last_sums.run(1)
    first_sums.run(5)
    last_sums.run(2)
    first_sums.run(6)
    stores[1].start()
    last_sums.run(3)

    total = jnp.zeros((C, C), F32)
    for p in range(2):
        for j in range(GRP):
            cols = pl.ds(C * j, C)
            grads = sums[block_at(8 * (1 + p) + j)].reshape(C, C)
            total += dot(grads, mix[p, :, cols], 1, 1)
    lift_mine[...] = total.astype(BF16)
    lift_copies = spread_rows(lift_mine, lift_parts, sem_lift, "grp")
    last_sums.run(4)
    lift_copies.wait_recv()
    stores[2].start()
    for copies in (lift_copies, *halos):
        copies.wait_send()
    last_sums.run(5)
    stores[3].start()
    last_sums.run(6)
    for copy in stores:
        copy.wait()


def finish_kernel(
    out_in,
    sums_in,
    taps_in,
    parts_in,
    lift_in,
    out_to,
    conv_to,
    lift_to,
    mix_to,
    proj_to,
    out,
    sums,
    taps,
    parts,
    own_rows,
    conv,
    lift,
    mix,
    proj,
    sems,
):
    def copies(first, *pairs):
        return [
            pltpu.make_async_copy(src, dst, sems.at[first + i])
            for i, (src, dst) in enumerate(pairs)
        ]

    cols = pl.ds(pl.multiple_of(spot("grp") * C, C), C)
    loads = copies(
        0,
        (taps_in, taps),
        (sums_in, sums),
        (parts_in, parts),
        (lift_in.at[:, cols], own_rows),
        (out_in, out),
    )
    stores = copies(5, (conv, conv_to), (lift, lift_to), (mix, mix_to), (proj, proj_to), (out, out_to))
    for copy in loads:
        copy.start()
    loads[0].wait()
    for c in range(3):
        for ab in range(9):
            conv[3 * ab + c] = taps[9 * c + ab].astype(F32).T
    stores[0].start()
    for copy in loads[1:4]:
        copy.wait()
    for j in range(GRP):
        cols = pl.ds(C * j, C)
        lift[:, cols] = sums[j].astype(F32) + parts[j].astype(F32)
        proj[j] = sums[24 + j].astype(F32)
        for p in range(2):
            mix[p, :, cols] = dot(own_rows[...], sums[8 * (1 + p) + j], 0, 0)
    for copy in stores[1:4]:
        copy.start()
    loads[4].wait()
    stores[4].start()
    for copy in stores:
        copy.wait()


def shards(
    field,
    sea,
    conv_weight,
    lift_weight,
    mix_weight,
    proj_weight,
    kx_modes,
    ky_modes,
    kz_modes,
    cotangent,
):
    smem = pl.BlockSpec(memory_space=pltpu.SMEM)
    hbm = pl.BlockSpec(memory_space=pl.ANY)
    out, sums, taps, lift_parts = pl.pallas_call(
        step_kernel,
        out_shape=(
            jax.ShapeDtypeStruct(field.shape, BF16),
            jax.ShapeDtypeStruct((2, 2, 4, 16, 16, C), BF16),
            jax.ShapeDtypeStruct((2, 2, 4, 16, 16, C), BF16),
            jax.ShapeDtypeStruct((GRP, C, C), BF16),
        ),
        in_specs=[hbm] * 7 + [smem] * 3,
        out_specs=(hbm,) * 4,
        scratch_shapes=[
            held(16, 16, 16, C),
            pltpu.VMEM((16, 16, 16), jnp.int32),
            held(4096, C, dtype=F32),
            held(16, 16, 16, C),
            held(3, 3, 3, C, C),
            held(C, W),
            held(2, C, W),
            held(W, C),
            pltpu.SemaphoreType.DMA((7,)),
            held(64, 256),
            held(32, 128),
            held(64, 128),
            held(64, 64),
            held(128, 128),
            held(18, 18, 16, C),
            held(3 * C, 4096),
            held(2, 16, 16, C),
            held(2, 16, 16, C),
            held(4, 16, C),
            held(9 * C, 3 * C),
            held(16, 256, C, dtype=F32),
            held(16, 256, C, dtype=F32),
            held(16, 256, C),
            held(512, 3 * C),
            held(512, C),
            held(C, C),
            held(GRP, C, C),
            held(GRP, C, C),
            held(C, C),
            held(2, GRP, C, C),
            held(3 * C, W),
            held(512, 256, dtype=F32),
            held(512, W),
            held(512, W),
            held(512, W),
            held(512, C, dtype=F32),
            held(8, 64, C, dtype=F32),
            held(3 * C, 9 * C),
            held(2, 2, 4, 16, 16, C),
            held(2, 2, 4, 16, 16, C),
            held(C, C),
            held(128, C, dtype=F32),
            held(16, 16, 16, C),
            held(2, 2, 4, 16, 16, C),
            held(2, 2, 4, 16, 16, C),
            held(GRP, C, C),
            pltpu.SemaphoreType.DMA((4,)),
            pltpu.SemaphoreType.DMA((3, 2)),
            pair_sems(),
            pair_sems(),
            pair_sems(),
            pair_sems(),
        ]
        + FILTER_SCRATCH()
        + FILTER_SCRATCH()
        + SUM_SCRATCH()
        + SUM_SCRATCH(),
        compiler_params=pltpu.CompilerParams(
            collective_id=1, has_side_effects=True, vmem_limit_bytes=56 * 2**20
        ),
        name="step",
    )(
        field,
        sea,
        cotangent,
        conv_weight,
        lift_weight,
        mix_weight,
        proj_weight,
        kx_modes,
        ky_modes,
        kz_modes,
    )
    out, conv, lift, mix, proj = pl.pallas_call(
        finish_kernel,
        out_shape=(
            jax.ShapeDtypeStruct(field.shape, BF16),
            jax.ShapeDtypeStruct((27, C, C), F32),
            jax.ShapeDtypeStruct((C, W), F32),
            jax.ShapeDtypeStruct((2, C, W), F32),
            jax.ShapeDtypeStruct((GRP, C, C), F32),
        ),
        in_specs=[hbm] * 5,
        out_specs=(hbm,) * 5,
        scratch_shapes=[
            held(16, 16, 16, C),
            held(32, C, C),
            held(32, C, C),
            held(GRP, C, C),
            held(C, C),
            held(27, C, C, dtype=F32),
            held(C, W, dtype=F32),
            held(2, C, W, dtype=F32),
            held(GRP, C, C, dtype=F32),
            pltpu.SemaphoreType.DMA((10,)),
        ],
        compiler_params=pltpu.CompilerParams(vmem_limit_bytes=56 * 2**20),
        name="finish",
    )(out, sums.reshape(32, C, C), taps.reshape(32, C, C), lift_parts, lift_weight)
    return (out, conv.reshape(3, 3, 3, C, C), lift, mix, proj.reshape(W, C))


def solution(mesh):
    return jax.shard_map(
        shards,
        mesh=mesh,
        in_specs=(
            P("tile", "grp", None, None),
            P("tile", "grp", None),
            P(),
            P(),
            P(None, "grp", None),
            P(),
            P(),
            P(),
            P(),
            P("tile", "grp", None, None),
        ),
        out_specs=(P("tile", "grp", None, None), P(), P(), P(None, "grp", None), P()),
        check_vma=False,
    )
```

```python
import math

import jax
import jax.numpy as jnp
from jax import lax
from jax.experimental import pallas as pl
from jax.experimental.pallas import tpu as pltpu
from jax.sharding import PartitionSpec as P

BX = 128
BY = 64
BZ = 8
KX = 32
KY = 32
KZ = 4
C = 128
W = 1024
GRP = 8
TILE = 16
PAIRS = 8
SCALE = 1.0 / math.sqrt(BX * BY * BZ * KX * KY * KZ)
ROOT = math.sqrt(2.0 / math.pi)
CUBE = 0.044715
F32 = jnp.float32
BF16 = jnp.bfloat16
MESH = pl.DeviceIdType.MESH


def dot(first, second, left=1, right=0):
    return lax.dot_general(
        first, second, (((left,), (right,)), ((), ())), preferred_element_type=F32
    )


def grid_of(shape, dim):
    return lax.broadcasted_iota(jnp.int32, shape, dim)


def cos_sin(turns, length):
    angles = (turns & (length - 1)).astype(F32) * (2.0 * math.pi / length)
    return jnp.cos(angles), jnp.sin(angles)


def z_table(kz):
    shape = (64, 128)
    row, lane = grid_of(shape, 0), grid_of(shape, 1)
    freq = jnp.concatenate([jnp.full((16, 128), kz[b], jnp.int32) for b in range(KZ)], 0)
    cosine, sine = cos_sin(freq * (lane & 7), BZ)
    p, s = (row >> 3) & 1, lane >> 6
    value = jnp.where(s == p, jnp.where(s == 0, cosine, -cosine), -sine)
    return jnp.where((row & 7) == ((lane >> 3) & 7), value, 0.0)


def y_table(ky, first):
    shape = (32, 128)
    row, lane = grid_of(shape, 0), grid_of(shape, 1)
    freq = jnp.zeros(shape, jnp.int32)
    for a in range(16):
        freq = jnp.where((row >> 1) == a, ky[first + a], freq)
    y = ((lane >> 4) << 3) + (lane & 7)
    cosine, sine = cos_sin(freq * y, BY)
    p, q = (lane >> 3) & 1, row & 1
    return jnp.where(p == q, cosine, jnp.where(q == 0, sine, -sine))


def x_table(kx):
    shape = (32, 256)
    row, lane = grid_of(shape, 0), grid_of(shape, 1)
    freq = jnp.zeros(shape, jnp.int32)
    for k in range(KX):
        freq = jnp.where(row == k, kx[k], freq)
    x = ((lane >> 4) << 3) + (lane & 7)
    cosine, sine = cos_sin(freq * x, BX)
    even = ((lane >> 3) & 1) == 0
    return jnp.concatenate(
        [jnp.where(even, cosine, sine), jnp.where(even, -sine, cosine)], 0
    )


def spot(axis):
    return lax.axis_index(axis)


def place():
    grp, tile = spot("grp"), spot("tile")
    return {
        "xlo": grp // 4,
        "y": lax.rem(grp, 4),
        "z": tile // 4,
        "xhi": lax.rem(tile // 2, 2),
        "core": lax.rem(tile, 2),
    }


LENGTHS = {"xlo": 2, "y": 4, "z": 4, "xhi": 2, "core": 2}
DIGITS = {
    "grp": ("xlo", "y"),
    "tile": ("z", "xhi", "core"),
    "ring_y": ("y",),
    "ring_z": ("z",),
    "xz": ("xlo", "z", "xhi"),
    "xy": ("xlo", "y", "xhi"),
}
HOPS = {"xlo": (0, 1), "y": (0, 1, 2, 1), "z": (0, 1, 2, 1), "xhi": (0, 2), "core": (0, 0)}


def digits_of(name, number):
    digits = {}
    for part in reversed(DIGITS[name]):
        digits[part] = number % LENGTHS[part]
        number //= LENGTHS[part]
    return digits


def size_of(name):
    return math.prod(LENGTHS[part] for part in DIGITS[name])


def own(name):
    here = place()
    index = 0
    for part in DIGITS[name]:
        index = index * LENGTHS[part] + here[part]
    return index


def group(name):
    def hops(away):
        return sum(HOPS[part][step] for part, step in digits_of(name, away).items())

    for away in sorted(range(1, size_of(name)), key=lambda away: (-hops(away), away)):
        there = place()
        index = 0
        for part, step in digits_of(name, away).items():
            if step:
                there[part] = lax.rem(there[part] + step, LENGTHS[part])
        for part in DIGITS[name]:
            index = index * LENGTHS[part] + there[part]
        device = {
            "grp": there["xlo"] * 4 + there["y"],
            "tile": there["z"] * 4 + there["xhi"] * 2 + there["core"],
        }
        yield away, index, device


def partner():
    tile = spot("tile")
    return {"tile": tile + 1 - 2 * lax.rem(tile, 2)}


def near(step_tile, step_grp):
    target = {}
    if step_tile:
        target["tile"] = lax.rem(spot("tile") + step_tile + TILE, TILE)
    if step_grp:
        target["grp"] = lax.rem(spot("grp") + step_grp + GRP, GRP)
    return target


DIAGONALS = ((1, 1), (1, -1), (-1, 1), (-1, -1))


def greet():
    barrier = pltpu.get_barrier_semaphore()
    targets = [device for name in ("grp", "tile") for _, _, device in group(name)]
    targets += [near(*step) for step in DIAGONALS]
    for away, _, device in group("xz"):
        steps = digits_of("xz", away)
        if steps["xlo"] and (steps["z"] or steps["xhi"]):
            targets.append(device)
    for away, _, device in group("xy"):
        steps = digits_of("xy", away)
        if steps["xhi"] and steps["y"]:
            targets.append(device)
    for device in targets:
        pl.semaphore_signal(barrier, inc=1, device_id=device, device_id_type=MESH)
    return lambda: pl.semaphore_wait(barrier, len(targets))


def remote(src, dst, sems, device):
    pltpu.make_async_remote_copy(
        src_ref=src,
        dst_ref=dst,
        send_sem=sems.at[0],
        recv_sem=sems.at[1],
        device_id=device,
        device_id_type=MESH,
    ).start()


class Sent:
    def __init__(self, all, sems):
        self.all, self.sems = all, sems

    def wait_send(self):
        pltpu.make_async_copy(self.all, self.all, self.sems.at[0]).wait()

    def wait_recv(self):
        pltpu.make_async_copy(self.all, self.all, self.sems.at[1]).wait()


def to_partner(src, dst, sems):
    remote(src, dst, sems, partner())
    return Sent(dst, sems)


def scatter_rows(src, slots, sems, name):
    for away, index, device in group(name):
        remote(src.at[index], slots.at[away], sems, device)
    return Sent(slots.at[pl.ds(1, size_of(name) - 1)], sems)


def add_rows(src, slots, copies, name):
    copies.wait_recv()
    total = src[own(name)].astype(F32)
    for away in range(1, size_of(name)):
        total += slots[away].astype(F32)
    return total.astype(BF16)


def exchange(src, dst, sems, name, share=1):
    me = own(name)
    for away, index, device in group(name):
        remote(src.at[index // share], dst.at[me], sems, device)
    dst[me] = src[me // share]
    return Sent(dst.at[pl.ds(1, size_of(name) - 1)], sems)


def spread_rows(src, dst, sems, name):
    me = own(name)
    for away, index, device in group(name):
        remote(src, dst.at[me], sems, device)
    dst[me] = src[...]
    return Sent(dst.at[pl.ds(1, size_of(name) - 1)], sems)


def pair_sems():
    return pltpu.SemaphoreType.DMA((2,))


def held(*shape, dtype=BF16):
    return pltpu.VMEM(shape, dtype)


FILTER_SCRATCH = (
    lambda: [held(KZ, 8, 16, C)]
    + [held(GRP, 8, 16, C) for _ in range(3)]
    + [held(TILE, 16, C) for _ in range(4)]
    + [held(256, C, dtype=F32)]
    + [pair_sems() for _ in range(4)]
)


def x_filter(y_tab, x_tab, work, beside):
    part, got_y, sent, back, mid, got, turned, home, wide, sem1, sem2, sem3, sem4 = work
    first = exchange(part, got_y, sem1, "grp", 2)
    beside[0]()
    first.wait_recv()
    for x in range(8):
        rows = got_y[:, x].reshape(128, C)
        wide[pl.ds(x, 32, stride=8), :] = dot(y_tab[...], rows)
    mid[...] = wide[...].astype(BF16).reshape(mid.shape)
    second = exchange(mid, got, sem2, "tile")
    beside[1]()
    second.wait_recv()
    modes = dot(x_tab[...], got[...].reshape(TILE * 16, C)).astype(BF16)
    turned[...] = dot(x_tab[...], modes, 0, 0).astype(BF16).reshape(turned.shape)
    third = exchange(turned, home, sem3, "tile")
    beside[2]()
    third.wait_recv()
    wide[...] = home[...].reshape(256, C).astype(F32)
    for x in range(8):
        rows = wide[pl.ds(x, 32, stride=8), :].astype(BF16)
        sent[:, x] = dot(y_tab[...], rows, 0, 0).astype(BF16).reshape(GRP, 16, C)
    fourth = exchange(sent, back, sem4, "grp")
    beside[3]()
    fourth.wait_recv()
    for copies in (first, second, third, fourth):
        copies.wait_send()


SUM_SCRATCH = (
    lambda: [held(2, 4, 16, 16, C) for _ in range(2)]
    + [held(4, 16, 16, C) for _ in range(2)]
    + [held(16, 16, C) for _ in range(4)]
    + [held(16, C) for _ in range(2)]
    + [held(16, 16, C) for _ in range(2)]
    + [pair_sems() for _ in range(10)]
)


class Sums:
    def __init__(self, x, y, last, work):
        self.x, self.y, self.last = x, y, last
        self.buffers, self.sems = work[:12], work[12:]
        self.sent = []

    def run(self, step):
        x, y, s = self.x, self.y, self.sems
        got, mine, sa, sb, ma, mb, ra, rb, ta, tb, ga, gb = self.buffers
        core = place()["core"]
        if step == 0:
            self.a = to_partner(x.at[1 - core], got, s[0])
        if step == 1:
            self.a.wait_recv()
            mine[...] = (x[core].astype(F32) + got[...].astype(F32)).astype(BF16)
            self.a = scatter_rows(mine.at[0], sa, s[1], "ring_y")
            self.b = scatter_rows(mine.at[1], sb, s[2], "ring_z")
        if step == 2:
            ma[...] = add_rows(mine.at[0], sa, self.a, "ring_y")
            self.a = scatter_rows(ma, ra, s[3], "xz")
            mb[...] = add_rows(mine.at[1], sb, self.b, "ring_z")
            self.b = scatter_rows(mb, rb, s[4], "xy")
        if step == 3:
            ta[...] = add_rows(ma, ra, self.a, "xz")
            self.a = spread_rows(ta, ga, s[5], "xz")
            tb[...] = add_rows(mb, rb, self.b, "xy")
            self.b = spread_rows(tb, gb, s[6], "xy")
        if step == 4:
            self.a.wait_recv()
            self.a = spread_rows(ga, y.at[core, 0], s[7], "ring_y")
            self.b.wait_recv()
            self.b = spread_rows(gb, y.at[core, 1], s[8], "ring_z")
        if step == 5:
            self.a.wait_recv()
            self.b.wait_recv()
            self.a = to_partner(y.at[core], self.last.at[core], s[9])
        if step == 6:
            self.a.wait_recv()
            for copies in self.sent:
                copies.wait_send()
            return
        self.sent += [self.a] if step in (0, 5) else [self.a, self.b]


def block_at(n):
    return n // 16, n // 8 % 2, n % 8 // 2, pl.ds(8 * (n % 2), 8)


def tanh_of(x):
    return jnp.tanh(ROOT * (x + CUBE * x * x * x))


def gelu_slope(x, t):
    return 0.5 * (1.0 + t) + 0.5 * x * (1.0 - t * t) * (ROOT * (1.0 + 3.0 * CUBE * x * x))


def shift_rows(rows, forward):
    z = lax.rem(lax.broadcasted_iota(jnp.int32, rows.shape, 0), 16)
    if forward:
        return jnp.where(z == 0, 0.0, pltpu.roll(rows, 1, 0))
    return jnp.where(z == 15, 0.0, pltpu.roll(rows, rows.shape[0] - 1, 0))


def pool(rows, tmp):
    tmp[...] = rows.reshape(8, 2, 16, C).sum(1).reshape(128, C)
    return tmp[pl.ds(0, 64, stride=2), :] + tmp[pl.ds(1, 64, stride=2), :]


def unpool(rows, tmp):
    tmp[pl.ds(0, 64, stride=2), :] = rows
    tmp[pl.ds(1, 64, stride=2), :] = rows
    wide = jnp.broadcast_to(tmp[...].reshape(8, 1, 16, C), (8, 2, 16, C))
    return wide.reshape(256, C)


def step_kernel(
    field_in,
    sea_in,
    cot_in,
    conv_in,
    lift_in,
    mix_in,
    proj_in,
    kx,
    ky,
    kz,
    out_to,
    sums_to,
    taps_to,
    lift_to,
    field,
    sea_wide,
    sea,
    cot,
    conv_w,
    lift,
    mix,
    proj,
    load_sems,
    x_tab,
    y_tab,
    z_tab,
    z_cells,
    z_twice,
    rim,
    upstream,
    halo_x,
    halo_y,
    halo_c,
    conv_flat,
    pre,
    base,
    hidden,
    feats,
    proj_grad,
    lift_own,
    lm_part,
    lm_slots,
    lm_mine,
    lm_all,
    stacked,
    bottle_pre,
    bottle_grad,
    bottle,
    bpg,
    direct,
    cell_grad,
    acc,
    sums_in,
    taps_in,
    lift_mine,
    tmp,
    out,
    sums,
    taps,
    lift_parts,
    store_sems,
    sem_halo,
    sem_lm1,
    sem_lm2,
    sem_lm3,
    sem_lift,
    *work,
):
    count = len(FILTER_SCRATCH())
    filter1, filter2 = work[:count], work[count : 2 * count]
    work = work[2 * count :]
    count = len(SUM_SCRATCH())
    first_sums = Sums(sums_in, sums, sums, work[:count])
    last_sums = Sums(taps_in, taps, taps_to, work[count:])
    grp, tile = spot("grp"), spot("tile")
    core = place()["core"]

    def sea_of(x):
        return sea[pl.ds(pl.multiple_of(256 * x, 256), 256), :].reshape(16, 16, C)

    loads = []
    for i, (src, dst) in enumerate(
        (
            (field_in, field),
            (sea_in, sea_wide),
            (conv_in, conv_w),
            (lift_in, lift),
            (mix_in, mix),
            (cot_in, cot),
            (proj_in, proj),
        )
    ):
        loads.append(pltpu.make_async_copy(src, dst, load_sems.at[i]))
        loads[i].start()
    stores = [
        pltpu.make_async_copy(src, dst, store_sems.at[i])
        for i, (src, dst) in enumerate(
            ((out, out_to), (sums, sums_to), (lift_parts, lift_to), (taps.at[core], taps_to.at[core]))
        )
    ]
    met = greet()
    x_tab[...] = x_table(kx).astype(BF16)
    y_tab[...] = y_table(ky, 16 * lax.rem(grp, 2)).astype(BF16)
    z_values = z_table(kz).astype(BF16)
    z_tab[...] = z_values
    z_cells[...] = z_values[:, :64]
    for j in range(GRP):
        z_twice[pl.ds(16 * j, 16), :] = z_values[16 * (j // 2) : 16 * (j // 2 + 1)]
    loads[1].wait()
    lines = sea_wide[...].reshape(256, 16).astype(F32).astype(BF16)
    for z in range(16):
        pick = (grid_of((16, C), 0) == z).astype(F32).astype(BF16)
        sea[pl.ds(z, 256, stride=16), :] = dot(lines, pick)
    loads[0].wait()

    @pl.loop(0, 16)
    def _(x):
        rim[x + 1, 1:17] = (field[x].astype(F32) * sea_of(x)).astype(BF16)

    met()

    inner = pl.ds(1, 16)
    strip_x, strip_y, corner = sem_halo.at[0], sem_halo.at[1], sem_halo.at[2]
    remote(rim.at[16, 16], halo_c.at[0], corner, near(1, 1))
    remote(rim.at[16, 1], halo_c.at[1], corner, near(1, -1))
    remote(rim.at[1, 16], halo_c.at[2], corner, near(-1, 1))
    remote(rim.at[1, 1], halo_c.at[3], corner, near(-1, -1))
    remote(rim.at[16, inner], halo_x.at[0], strip_x, near(1, 0))
    remote(rim.at[1, inner], halo_x.at[1], strip_x, near(-1, 0))
    remote(rim.at[inner, 16], halo_y.at[0], strip_y, near(0, 1))
    remote(rim.at[inner, 1], halo_y.at[1], strip_y, near(0, -1))
    halos = (Sent(halo_c, corner), Sent(halo_x, strip_x), Sent(halo_y, strip_y))
    for copy in loads[2:]:
        copy.wait()
    lift_own[...] = lift[:, pl.ds(pl.multiple_of(grp * C, C), C)]
    product = dot(lift_own[...], mix[core]).astype(BF16)
    for j in range(GRP):
        lm_part[j] = product[:, C * j : C * (j + 1)]

    for a in range(3):
        for b in range(3):
            for c in range(3):
                conv_flat[pl.ds(C * (3 * a + b), C), pl.ds(C * c, C)] = conv_w[a, b, c]

    def convolve(*boxes):
        window = jnp.concatenate(
            [
                jnp.concatenate(
                    [
                        rim[pl.ds(x + a, nx), pl.ds(y + b, ny)].reshape(16 * nx * ny, C)
                        for x, nx, y, ny in boxes
                    ],
                    0,
                )
                for a in range(3)
                for b in range(3)
            ],
            1,
        )
        product = dot(window, conv_flat[...])
        rows = (
            product[:, C : 2 * C]
            + shift_rows(product[:, :C], True)
            + shift_rows(product[:, 2 * C :], False)
        )
        active = (0.5 * rows * (1.0 + tanh_of(rows))).astype(BF16)
        done = 0
        for x, nx, y, ny in boxes:
            count = 16 * nx * ny
            shape = (nx, ny, 16, C)
            pre[pl.ds(x, nx), pl.ds(y, ny)] = rows[done : done + count].reshape(shape)
            hidden[pl.ds(x, nx), pl.ds(y, ny)] = active[done : done + count].reshape(shape)
            done += count

    convolve((1, 14, 1, 14))

    @pl.loop(0, 8)
    def _(i):
        total = cot[2 * i].astype(F32) * sea_of(2 * i)
        total += cot[2 * i + 1].astype(F32) * sea_of(2 * i + 1)
        rows = pool(total.reshape(256, C), tmp)
        proj_grad[pl.ds(pl.multiple_of(64 * i, 64), 64), :] = rows.astype(BF16)

    stacked[pl.ds(0, C), :] = lift[...]
    for copies in halos:
        copies.wait_recv()
    lm_first = scatter_rows(lm_part, lm_slots, sem_lm1, "grp")
    sides = (tile > 0, tile < TILE - 1, grp > 0, grp < GRP - 1)

    def keep(flag, rows):
        return jnp.where(flag, rows, jnp.zeros_like(rows))

    for side, x in ((0, 0), (1, 17)):
        rim[x, 1:17] = keep(sides[side], halo_x[side])
    for side, y in ((0, 0), (1, 17)):
        rim[1:17, y] = keep(sides[2 + side], halo_y[side])
    for i, x, y in ((0, 0, 0), (1, 0, 17), (2, 17, 0), (3, 17, 17)):
        flag = jnp.logical_and(sides[0 if x == 0 else 1], sides[2 if y == 0 else 3])
        rim[x, y] = keep(flag, halo_c[i])

    def windows():
        return jnp.concatenate(
            [rim[pl.ds(a, 16), b : b + 16].reshape(4096, C) for a in range(3) for b in range(3)], 1
        )

    convolve((0, 1, 0, 16), (15, 1, 0, 16), (1, 14, 0, 1), (1, 14, 15, 1))

    for i in range(8):
        total = hidden[2 * i].astype(F32) + hidden[2 * i + 1].astype(F32)
        coarse = (0.125 * pool(total.reshape(256, C), tmp)).astype(BF16)
        feats[pl.ds(64 * i, 64), pl.ds(0, C)] = coarse
        filter1[0][:, i] = dot(z_cells[...], coarse).astype(BF16).reshape(KZ, 16, C)

    def back_through():
        for j in range(4):
            cols = pl.ds(256 * j, 256)
            bottle_grad[:, cols] = dot(proj_grad[...], proj[cols, :], 1, 1).astype(BF16)

    lm = {}

    def gather_lm():
        lm_mine[...] = add_rows(lm_part, lm_slots, lm_first, "grp")
        lm["grp"] = spread_rows(lm_mine, lm_all.at[core], sem_lm2, "grp")
        back_through()

    def swap_lm():
        lm["grp"].wait_recv()
        lm["core"] = to_partner(lm_all.at[core], lm_all.at[core], sem_lm3)

    def slopes():
        @pl.loop(0, 16)
        def _(x):
            value = pre[x].reshape(256, C)
            slope = gelu_slope(value, tanh_of(value))
            pre[x] = slope.reshape(16, 16, C)
            base[x] = slope * (cot[x].astype(F32) * sea_of(x)).reshape(256, C)

    x_filter(y_tab, x_tab, filter1, (lambda: None, gather_lm, slopes, swap_lm))

    lm["core"].wait_recv()
    for p in range(2):
        for j in range(GRP):
            stacked[pl.ds(C * (p + 1), C), pl.ds(C * j, C)] = lm_all[p, j]
    for copies in (lm_first, lm["grp"], lm["core"]):
        copies.wait_send()

    for i in range(8):
        modes = filter1[3][:, i].reshape(128, C)
        both = (SCALE * dot(z_twice[...], modes, 0, 0)).astype(BF16)
        feats[pl.ds(64 * i, 64), pl.ds(C, C)] = both[:64]
        feats[pl.ds(64 * i, 64), pl.ds(2 * C, C)] = both[64:]

    for j in range(4):
        cols = pl.ds(256 * j, 256)
        bottle_pre[...] = dot(feats[...], stacked[:, cols])

        @pl.loop(0, 8)
        def _(r):
            rows = pl.ds(pl.multiple_of(64 * r, 64), 64)
            v = bottle_pre[rows, :]
            t = tanh_of(v)
            bottle[rows, cols] = (0.5 * v * (1.0 + t)).astype(BF16)
            bpg[rows, cols] = (bottle_grad[rows, cols].astype(F32) * gelu_slope(v, t)).astype(BF16)

    feats_grad = dot(bpg[...], stacked[...], 1, 1)
    direct[...] = feats_grad[:, :C]
    pair_grad = (SCALE * feats_grad[:, C:]).astype(BF16)
    for i in range(8):
        rows = pair_grad[64 * i : 64 * (i + 1)]
        stacked_rows = jnp.concatenate([rows[:, :C], rows[:, C:]], 0)
        filter2[0][:, i] = dot(z_tab[...], stacked_rows).astype(BF16).reshape(KZ, 16, C)

    def weight_sums():
        for j in range(GRP):
            cols = pl.ds(C * j, C)
            outer = dot(feats[...], bpg[:, cols], 0, 0).astype(BF16)
            for k in range(3):
                rows = outer[C * k : C * (k + 1)]
                sums_in[block_at(8 * k + j)] = rows.reshape(8, 16, C)
            rows = dot(bottle[:, cols], proj_grad[...], 0, 0).astype(BF16)
            sums_in[block_at(24 + j)] = rows.reshape(8, 16, C)
        first_sums.run(0)

    def write_cells():
        direct_out = dot(bottle[...], proj[...])
        for i in range(8):
            cell_grad[i] = direct_out[64 * i : 64 * (i + 1)]

        @pl.loop(0, 8)
        def _(i):
            spread = unpool(cell_grad[i], tmp)
            for half in range(2):
                x = 2 * i + half
                value = hidden[x].astype(F32) + spread.reshape(16, 16, C)
                out[x] = (value * sea_of(x)).astype(BF16)

        stores[0].start()

    x_filter(
        y_tab,
        x_tab,
        filter2,
        (weight_sums, lambda: first_sums.run(1), write_cells, lambda: first_sums.run(2)),
    )

    for i in range(8):
        modes = filter2[3][:, i].reshape(128, C)
        rows = dot(z_twice[...], modes, 0, 0)[:64] + direct[pl.ds(64 * i, 64), :]
        cell_grad[i] = 0.125 * rows

    first_sums.run(3)

    @pl.loop(0, 8)
    def _(i):
        spread = unpool(cell_grad[i], tmp)
        for half in range(2):
            x = 2 * i + half
            grad = (base[x] + spread * pre[x].reshape(256, C)).astype(BF16).astype(F32)
            shifted = jnp.concatenate(
                [shift_rows(grad, False), grad, shift_rows(grad, True)], 1
            ).astype(BF16)
            upstream[:, pl.ds(pl.multiple_of(256 * x, 256), 256)] = shifted.T

    acc[...] = dot(upstream[...], windows()).astype(BF16)
    for c in range(3):
        for ab in range(9):
            rows = acc[pl.ds(C * c, C), pl.ds(C * ab, C)]
            taps_in[block_at(9 * c + ab)] = rows.reshape(8, 16, C)
    for n in range(27, 32):
        taps_in[block_at(n)] = jnp.zeros((8, 16, C), BF16)
    last_sums.run(0)
    first_sums.run(4)
    last_sums.run(1)
    first_sums.run(5)
    last_sums.run(2)
    first_sums.run(6)
    stores[1].start()
    last_sums.run(3)

    total = jnp.zeros((C, C), F32)
    for p in range(2):
        for j in range(GRP):
            cols = pl.ds(C * j, C)
            grads = sums[block_at(8 * (1 + p) + j)].reshape(C, C)
            total += dot(grads, mix[p, :, cols], 1, 1)
    lift_mine[...] = total.astype(BF16)
    lift_copies = spread_rows(lift_mine, lift_parts, sem_lift, "grp")
    last_sums.run(4)
    lift_copies.wait_recv()
    stores[2].start()
    for copies in (lift_copies, *halos):
        copies.wait_send()
    last_sums.run(5)
    stores[3].start()
    last_sums.run(6)
    for copy in stores:
        copy.wait()


def finish_kernel(
    out_in,
    sums_in,
    taps_in,
    parts_in,
    lift_in,
    out_to,
    conv_to,
    lift_to,
    mix_to,
    proj_to,
    out,
    sums,
    taps,
    parts,
    own_rows,
    conv,
    lift,
    mix,
    proj,
    sems,
):
    def copies(first, *pairs):
        return [
            pltpu.make_async_copy(src, dst, sems.at[first + i])
            for i, (src, dst) in enumerate(pairs)
        ]

    cols = pl.ds(pl.multiple_of(spot("grp") * C, C), C)
    loads = copies(
        0,
        (taps_in, taps),
        (sums_in, sums),
        (parts_in, parts),
        (lift_in.at[:, cols], own_rows),
        (out_in, out),
    )
    stores = copies(5, (conv, conv_to), (lift, lift_to), (mix, mix_to), (proj, proj_to), (out, out_to))
    for copy in loads:
        copy.start()
    loads[0].wait()
    for c in range(3):
        for ab in range(9):
            conv[3 * ab + c] = taps[9 * c + ab].astype(F32).T
    stores[0].start()
    for copy in loads[1:4]:
        copy.wait()
    for j in range(GRP):
        cols = pl.ds(C * j, C)
        lift[:, cols] = sums[j].astype(F32) + parts[j].astype(F32)
        proj[j] = sums[24 + j].astype(F32)
        for p in range(2):
            mix[p, :, cols] = dot(own_rows[...], sums[8 * (1 + p) + j], 0, 0)
    for copy in stores[1:4]:
        copy.start()
    loads[4].wait()
    stores[4].start()
    for copy in stores:
        copy.wait()


def shards(
    field,
    sea,
    conv_weight,
    lift_weight,
    mix_weight,
    proj_weight,
    kx_modes,
    ky_modes,
    kz_modes,
    cotangent,
):
    smem = pl.BlockSpec(memory_space=pltpu.SMEM)
    hbm = pl.BlockSpec(memory_space=pl.ANY)
    out, sums, taps, lift_parts = pl.pallas_call(
        step_kernel,
        out_shape=(
            jax.ShapeDtypeStruct(field.shape, BF16),
            jax.ShapeDtypeStruct((2, 2, 4, 16, 16, C), BF16),
            jax.ShapeDtypeStruct((2, 2, 4, 16, 16, C), BF16),
            jax.ShapeDtypeStruct((GRP, C, C), BF16),
        ),
        in_specs=[hbm] * 7 + [smem] * 3,
        out_specs=(hbm,) * 4,
        scratch_shapes=[
            held(16, 16, 16, C),
            pltpu.VMEM((16, 16, 16), jnp.int32),
            held(4096, C, dtype=F32),
            held(16, 16, 16, C),
            held(3, 3, 3, C, C),
            held(C, W),
            held(2, C, W),
            held(W, C),
            pltpu.SemaphoreType.DMA((7,)),
            held(64, 256),
            held(32, 128),
            held(64, 128),
            held(64, 64),
            held(128, 128),
            held(18, 18, 16, C),
            held(3 * C, 4096),
            held(2, 16, 16, C),
            held(2, 16, 16, C),
            held(4, 16, C),
            held(9 * C, 3 * C),
            held(16, 16, 16, C, dtype=F32),
            held(16, 256, C, dtype=F32),
            held(16, 16, 16, C),
            held(512, 3 * C),
            held(512, C),
            held(C, C),
            held(GRP, C, C),
            held(GRP, C, C),
            held(C, C),
            held(2, GRP, C, C),
            held(3 * C, W),
            held(512, 256, dtype=F32),
            held(512, W),
            held(512, W),
            held(512, W),
            held(512, C, dtype=F32),
            held(8, 64, C, dtype=F32),
            held(3 * C, 9 * C),
            held(2, 2, 4, 16, 16, C),
            held(2, 2, 4, 16, 16, C),
            held(C, C),
            held(128, C, dtype=F32),
            held(16, 16, 16, C),
            held(2, 2, 4, 16, 16, C),
            held(2, 2, 4, 16, 16, C),
            held(GRP, C, C),
            pltpu.SemaphoreType.DMA((4,)),
            pltpu.SemaphoreType.DMA((3, 2)),
            pair_sems(),
            pair_sems(),
            pair_sems(),
            pair_sems(),
        ]
        + FILTER_SCRATCH()
        + FILTER_SCRATCH()
        + SUM_SCRATCH()
        + SUM_SCRATCH(),
        compiler_params=pltpu.CompilerParams(
            collective_id=1, has_side_effects=True, vmem_limit_bytes=56 * 2**20
        ),
        name="step",
    )(
        field,
        sea,
        cotangent,
        conv_weight,
        lift_weight,
        mix_weight,
        proj_weight,
        kx_modes,
        ky_modes,
        kz_modes,
    )
    out, conv, lift, mix, proj = pl.pallas_call(
        finish_kernel,
        out_shape=(
            jax.ShapeDtypeStruct(field.shape, BF16),
            jax.ShapeDtypeStruct((27, C, C), F32),
            jax.ShapeDtypeStruct((C, W), F32),
            jax.ShapeDtypeStruct((2, C, W), F32),
            jax.ShapeDtypeStruct((GRP, C, C), F32),
        ),
        in_specs=[hbm] * 5,
        out_specs=(hbm,) * 5,
        scratch_shapes=[
            held(16, 16, 16, C),
            held(32, C, C),
            held(32, C, C),
            held(GRP, C, C),
            held(C, C),
            held(27, C, C, dtype=F32),
            held(C, W, dtype=F32),
            held(2, C, W, dtype=F32),
            held(GRP, C, C, dtype=F32),
            pltpu.SemaphoreType.DMA((10,)),
        ],
        compiler_params=pltpu.CompilerParams(vmem_limit_bytes=56 * 2**20),
        name="finish",
    )(out, sums.reshape(32, C, C), taps.reshape(32, C, C), lift_parts, lift_weight)
    return (out, conv.reshape(3, 3, 3, C, C), lift, mix, proj.reshape(W, C))


def solution(mesh):
    return jax.shard_map(
        shards,
        mesh=mesh,
        in_specs=(
            P("tile", "grp", None, None),
            P("tile", "grp", None),
            P(),
            P(),
            P(None, "grp", None),
            P(),
            P(),
            P(),
            P(),
            P("tile", "grp", None, None),
        ),
        out_specs=(P("tile", "grp", None, None), P(), P(), P(None, "grp", None), P()),
        check_vma=False,
    )
```

```python
import math

import jax
import jax.numpy as jnp
from jax import lax
from jax.experimental import pallas as pl
from jax.experimental.pallas import tpu as pltpu
from jax.sharding import PartitionSpec as P

BX = 128
BY = 64
BZ = 8
KX = 32
KY = 32
KZ = 4
C = 128
W = 1024
GRP = 8
TILE = 16
PAIRS = 8
SCALE = 1.0 / math.sqrt(BX * BY * BZ * KX * KY * KZ)
ROOT = math.sqrt(2.0 / math.pi)
CUBE = 0.044715
F32 = jnp.float32
BF16 = jnp.bfloat16
MESH = pl.DeviceIdType.MESH


def dot(first, second, left=1, right=0):
    return lax.dot_general(
        first, second, (((left,), (right,)), ((), ())), preferred_element_type=F32
    )


def grid_of(shape, dim):
    return lax.broadcasted_iota(jnp.int32, shape, dim)


def cos_sin(turns, length):
    angles = (turns & (length - 1)).astype(F32) * (2.0 * math.pi / length)
    return jnp.cos(angles), jnp.sin(angles)


def z_table(kz):
    shape = (64, 128)
    row, lane = grid_of(shape, 0), grid_of(shape, 1)
    freq = jnp.concatenate([jnp.full((16, 128), kz[b], jnp.int32) for b in range(KZ)], 0)
    cosine, sine = cos_sin(freq * (lane & 7), BZ)
    p, s = (row >> 3) & 1, lane >> 6
    value = jnp.where(s == p, jnp.where(s == 0, cosine, -cosine), -sine)
    return jnp.where((row & 7) == ((lane >> 3) & 7), value, 0.0)


def y_table(ky, first):
    shape = (32, 128)
    row, lane = grid_of(shape, 0), grid_of(shape, 1)
    freq = jnp.zeros(shape, jnp.int32)
    for a in range(16):
        freq = jnp.where((row >> 1) == a, ky[first + a], freq)
    y = ((lane >> 4) << 3) + (lane & 7)
    cosine, sine = cos_sin(freq * y, BY)
    p, q = (lane >> 3) & 1, row & 1
    return jnp.where(p == q, cosine, jnp.where(q == 0, sine, -sine))


def x_table(kx):
    shape = (32, 256)
    row, lane = grid_of(shape, 0), grid_of(shape, 1)
    freq = jnp.zeros(shape, jnp.int32)
    for k in range(KX):
        freq = jnp.where(row == k, kx[k], freq)
    x = ((lane >> 4) << 3) + (lane & 7)
    cosine, sine = cos_sin(freq * x, BX)
    even = ((lane >> 3) & 1) == 0
    return jnp.concatenate(
        [jnp.where(even, cosine, sine), jnp.where(even, -sine, cosine)], 0
    )


def spot(axis):
    return lax.axis_index(axis)


def place():
    grp, tile = spot("grp"), spot("tile")
    return {
        "xlo": grp // 4,
        "y": lax.rem(grp, 4),
        "z": tile // 4,
        "xhi": lax.rem(tile // 2, 2),
        "core": lax.rem(tile, 2),
    }


LENGTHS = {"xlo": 2, "y": 4, "z": 4, "xhi": 2, "core": 2}
DIGITS = {
    "grp": ("xlo", "y"),
    "tile": ("z", "xhi", "core"),
    "ring_y": ("y",),
    "ring_z": ("z",),
    "xz": ("xlo", "z", "xhi"),
    "xy": ("xlo", "y", "xhi"),
}
HOPS = {"xlo": (0, 1), "y": (0, 1, 2, 1), "z": (0, 1, 2, 1), "xhi": (0, 2), "core": (0, 0)}


def digits_of(name, number):
    digits = {}
    for part in reversed(DIGITS[name]):
        digits[part] = number % LENGTHS[part]
        number //= LENGTHS[part]
    return digits


def size_of(name):
    return math.prod(LENGTHS[part] for part in DIGITS[name])


def own(name):
    here = place()
    index = 0
    for part in DIGITS[name]:
        index = index * LENGTHS[part] + here[part]
    return index


def group(name):
    def hops(away):
        return sum(HOPS[part][step] for part, step in digits_of(name, away).items())

    for away in sorted(range(1, size_of(name)), key=lambda away: (-hops(away), away)):
        there = place()
        index = 0
        for part, step in digits_of(name, away).items():
            if step:
                there[part] = lax.rem(there[part] + step, LENGTHS[part])
        for part in DIGITS[name]:
            index = index * LENGTHS[part] + there[part]
        device = {
            "grp": there["xlo"] * 4 + there["y"],
            "tile": there["z"] * 4 + there["xhi"] * 2 + there["core"],
        }
        yield away, index, device


def partner():
    tile = spot("tile")
    return {"tile": tile + 1 - 2 * lax.rem(tile, 2)}


def near(step_tile, step_grp):
    target = {}
    if step_tile:
        target["tile"] = lax.rem(spot("tile") + step_tile + TILE, TILE)
    if step_grp:
        target["grp"] = lax.rem(spot("grp") + step_grp + GRP, GRP)
    return target


DIAGONALS = ((1, 1), (1, -1), (-1, 1), (-1, -1))


def greet():
    barrier = pltpu.get_barrier_semaphore()
    targets = [device for name in ("grp", "tile") for _, _, device in group(name)]
    targets += [near(*step) for step in DIAGONALS]
    for away, _, device in group("xz"):
        steps = digits_of("xz", away)
        if steps["xlo"] and (steps["z"] or steps["xhi"]):
            targets.append(device)
    for away, _, device in group("xy"):
        steps = digits_of("xy", away)
        if steps["xhi"] and steps["y"]:
            targets.append(device)
    for device in targets:
        pl.semaphore_signal(barrier, inc=1, device_id=device, device_id_type=MESH)
    return lambda: pl.semaphore_wait(barrier, len(targets))


def remote(src, dst, sems, device):
    pltpu.make_async_remote_copy(
        src_ref=src,
        dst_ref=dst,
        send_sem=sems.at[0],
        recv_sem=sems.at[1],
        device_id=device,
        device_id_type=MESH,
    ).start()


class Sent:
    def __init__(self, all, sems):
        self.all, self.sems = all, sems

    def wait_send(self):
        pltpu.make_async_copy(self.all, self.all, self.sems.at[0]).wait()

    def wait_recv(self):
        pltpu.make_async_copy(self.all, self.all, self.sems.at[1]).wait()


def to_partner(src, dst, sems):
    remote(src, dst, sems, partner())
    return Sent(dst, sems)


def scatter_rows(src, slots, sems, name):
    for away, index, device in group(name):
        remote(src.at[index], slots.at[away], sems, device)
    return Sent(slots.at[pl.ds(1, size_of(name) - 1)], sems)


def add_rows(src, slots, copies, name):
    copies.wait_recv()
    total = src[own(name)].astype(F32)
    for away in range(1, size_of(name)):
        total += slots[away].astype(F32)
    return total.astype(BF16)


def exchange(src, dst, sems, name, share=1):
    me = own(name)
    for away, index, device in group(name):
        remote(src.at[index // share], dst.at[me], sems, device)
    dst[me] = src[me // share]
    return Sent(dst.at[pl.ds(1, size_of(name) - 1)], sems)


def spread_rows(src, dst, sems, name):
    me = own(name)
    for away, index, device in group(name):
        remote(src, dst.at[me], sems, device)
    dst[me] = src[...]
    return Sent(dst.at[pl.ds(1, size_of(name) - 1)], sems)


def pair_sems():
    return pltpu.SemaphoreType.DMA((2,))


def held(*shape, dtype=BF16):
    return pltpu.VMEM(shape, dtype)


FILTER_SCRATCH = (
    lambda: [held(KZ, 8, 16, C)]
    + [held(GRP, 8, 16, C) for _ in range(3)]
    + [held(TILE, 16, C) for _ in range(4)]
    + [held(256, C, dtype=F32)]
    + [pair_sems() for _ in range(4)]
)


def x_filter(y_tab, x_tab, work, beside):
    part, got_y, sent, back, mid, got, turned, home, wide, sem1, sem2, sem3, sem4 = work
    first = exchange(part, got_y, sem1, "grp", 2)
    beside[0]()
    first.wait_recv()
    for x in range(8):
        rows = got_y[:, x].reshape(128, C)
        wide[pl.ds(x, 32, stride=8), :] = dot(y_tab[...], rows)
    mid[...] = wide[...].astype(BF16).reshape(mid.shape)
    second = exchange(mid, got, sem2, "tile")
    beside[1]()
    second.wait_recv()
    modes = dot(x_tab[...], got[...].reshape(TILE * 16, C)).astype(BF16)
    turned[...] = dot(x_tab[...], modes, 0, 0).astype(BF16).reshape(turned.shape)
    third = exchange(turned, home, sem3, "tile")
    beside[2]()
    third.wait_recv()
    wide[...] = home[...].reshape(256, C).astype(F32)
    for x in range(8):
        rows = wide[pl.ds(x, 32, stride=8), :].astype(BF16)
        sent[:, x] = dot(y_tab[...], rows, 0, 0).astype(BF16).reshape(GRP, 16, C)
    fourth = exchange(sent, back, sem4, "grp")
    beside[3]()
    fourth.wait_recv()
    for copies in (first, second, third, fourth):
        copies.wait_send()


SUM_SCRATCH = (
    lambda: [held(2, 4, 16, 16, C) for _ in range(2)]
    + [held(4, 16, 16, C) for _ in range(2)]
    + [held(16, 16, C) for _ in range(4)]
    + [held(16, C) for _ in range(2)]
    + [held(16, 16, C) for _ in range(2)]
    + [pair_sems() for _ in range(10)]
)


class Sums:
    def __init__(self, x, y, last, work):
        self.x, self.y, self.last = x, y, last
        self.buffers, self.sems = work[:12], work[12:]
        self.sent = []

    def run(self, step):
        x, y, s = self.x, self.y, self.sems
        got, mine, sa, sb, ma, mb, ra, rb, ta, tb, ga, gb = self.buffers
        core = place()["core"]
        if step == 0:
            self.a = to_partner(x.at[1 - core], got, s[0])
        if step == 1:
            self.a.wait_recv()
            mine[...] = (x[core].astype(F32) + got[...].astype(F32)).astype(BF16)
            self.a = scatter_rows(mine.at[0], sa, s[1], "ring_y")
            self.b = scatter_rows(mine.at[1], sb, s[2], "ring_z")
        if step == 2:
            ma[...] = add_rows(mine.at[0], sa, self.a, "ring_y")
            self.a = scatter_rows(ma, ra, s[3], "xz")
            mb[...] = add_rows(mine.at[1], sb, self.b, "ring_z")
            self.b = scatter_rows(mb, rb, s[4], "xy")
        if step == 3:
            ta[...] = add_rows(ma, ra, self.a, "xz")
            self.a = spread_rows(ta, ga, s[5], "xz")
            tb[...] = add_rows(mb, rb, self.b, "xy")
            self.b = spread_rows(tb, gb, s[6], "xy")
        if step == 4:
            self.a.wait_recv()
            self.a = spread_rows(ga, y.at[core, 0], s[7], "ring_y")
            self.b.wait_recv()
            self.b = spread_rows(gb, y.at[core, 1], s[8], "ring_z")
        if step == 5:
            self.a.wait_recv()
            self.b.wait_recv()
            self.a = to_partner(y.at[core], self.last.at[core], s[9])
        if step == 6:
            self.a.wait_recv()
            for copies in self.sent:
                copies.wait_send()
            return
        self.sent += [self.a] if step in (0, 5) else [self.a, self.b]


def block_at(n):
    return n // 16, n // 8 % 2, n % 8 // 2, pl.ds(8 * (n % 2), 8)


def tanh_of(x):
    return jnp.tanh(ROOT * (x + CUBE * x * x * x))


def gelu_slope(x, t):
    return 0.5 * (1.0 + t) + 0.5 * x * (1.0 - t * t) * (ROOT * (1.0 + 3.0 * CUBE * x * x))


def shift_rows(rows, forward):
    z = lax.rem(lax.broadcasted_iota(jnp.int32, rows.shape, 0), 16)
    if forward:
        return jnp.where(z == 0, 0.0, pltpu.roll(rows, 1, 0))
    return jnp.where(z == 15, 0.0, pltpu.roll(rows, rows.shape[0] - 1, 0))


def pool(rows, tmp):
    tmp[...] = rows.reshape(8, 2, 16, C).sum(1).reshape(128, C)
    return tmp[pl.ds(0, 64, stride=2), :] + tmp[pl.ds(1, 64, stride=2), :]


def unpool(rows, tmp):
    tmp[pl.ds(0, 64, stride=2), :] = rows
    tmp[pl.ds(1, 64, stride=2), :] = rows
    wide = jnp.broadcast_to(tmp[...].reshape(8, 1, 16, C), (8, 2, 16, C))
    return wide.reshape(256, C)


def step_kernel(
    field_in,
    sea_in,
    cot_in,
    conv_in,
    lift_in,
    mix_in,
    proj_in,
    kx,
    ky,
    kz,
    out_to,
    sums_to,
    taps_to,
    lift_to,
    field,
    sea_wide,
    sea,
    cot,
    conv_w,
    lift,
    mix,
    proj,
    load_sems,
    x_tab,
    y_tab,
    z_tab,
    z_cells,
    z_twice,
    rim,
    upstream,
    halo_x,
    halo_y,
    halo_c,
    conv_flat,
    pre,
    base,
    hidden,
    feats,
    proj_grad,
    lift_own,
    lm_part,
    lm_slots,
    lm_mine,
    lm_all,
    stacked,
    bottle_pre,
    bottle_grad,
    bottle,
    bpg,
    direct,
    cell_grad,
    acc,
    sums_in,
    taps_in,
    lift_mine,
    tmp,
    out,
    sums,
    taps,
    lift_parts,
    store_sems,
    sem_halo,
    sem_lm1,
    sem_lm2,
    sem_lm3,
    sem_lift,
    *work,
):
    count = len(FILTER_SCRATCH())
    filter1, filter2 = work[:count], work[count : 2 * count]
    work = work[2 * count :]
    count = len(SUM_SCRATCH())
    first_sums = Sums(sums_in, sums, sums, work[:count])
    last_sums = Sums(taps_in, taps, taps_to, work[count:])
    grp, tile = spot("grp"), spot("tile")
    core = place()["core"]

    def sea_of(x):
        return sea[pl.ds(pl.multiple_of(256 * x, 256), 256), :].reshape(16, 16, C)

    loads = []
    for i, (src, dst) in enumerate(
        (
            (field_in, field),
            (sea_in, sea_wide),
            (conv_in, conv_w),
            (lift_in, lift),
            (mix_in, mix),
            (cot_in, cot),
            (proj_in, proj),
        )
    ):
        loads.append(pltpu.make_async_copy(src, dst, load_sems.at[i]))
        loads[i].start()
    stores = [
        pltpu.make_async_copy(src, dst, store_sems.at[i])
        for i, (src, dst) in enumerate(
            ((out, out_to), (sums, sums_to), (lift_parts, lift_to), (taps.at[core], taps_to.at[core]))
        )
    ]
    met = greet()
    x_tab[...] = x_table(kx).astype(BF16)
    y_tab[...] = y_table(ky, 16 * lax.rem(grp, 2)).astype(BF16)
    z_values = z_table(kz).astype(BF16)
    z_tab[...] = z_values
    z_cells[...] = z_values[:, :64]
    for j in range(GRP):
        z_twice[pl.ds(16 * j, 16), :] = z_values[16 * (j // 2) : 16 * (j // 2 + 1)]
    loads[1].wait()
    lines = sea_wide[...].reshape(256, 16).astype(F32).astype(BF16)
    for z in range(16):
        pick = (grid_of((16, C), 0) == z).astype(F32).astype(BF16)
        sea[pl.ds(z, 256, stride=16), :] = dot(lines, pick)
    loads[0].wait()

    @pl.loop(0, 16)
    def _(x):
        rim[x + 1, 1:17] = (field[x].astype(F32) * sea_of(x)).astype(BF16)

    met()

    inner = pl.ds(1, 16)
    strip_x, strip_y, corner = sem_halo.at[0], sem_halo.at[1], sem_halo.at[2]
    remote(rim.at[16, 16], halo_c.at[0], corner, near(1, 1))
    remote(rim.at[16, 1], halo_c.at[1], corner, near(1, -1))
    remote(rim.at[1, 16], halo_c.at[2], corner, near(-1, 1))
    remote(rim.at[1, 1], halo_c.at[3], corner, near(-1, -1))
    remote(rim.at[16, inner], halo_x.at[0], strip_x, near(1, 0))
    remote(rim.at[1, inner], halo_x.at[1], strip_x, near(-1, 0))
    remote(rim.at[inner, 16], halo_y.at[0], strip_y, near(0, 1))
    remote(rim.at[inner, 1], halo_y.at[1], strip_y, near(0, -1))
    halos = (Sent(halo_c, corner), Sent(halo_x, strip_x), Sent(halo_y, strip_y))
    for copy in loads[2:]:
        copy.wait()
    lift_own[...] = lift[:, pl.ds(pl.multiple_of(grp * C, C), C)]
    product = dot(lift_own[...], mix[core]).astype(BF16)
    for j in range(GRP):
        lm_part[j] = product[:, C * j : C * (j + 1)]

    for a in range(3):
        for b in range(3):
            for c in range(3):
                conv_flat[pl.ds(C * (3 * a + b), C), pl.ds(C * c, C)] = conv_w[a, b, c]

    def convolve(*boxes):
        window = jnp.concatenate(
            [
                jnp.concatenate(
                    [
                        rim[pl.ds(x + a, nx), pl.ds(y + b, ny)].reshape(16 * nx * ny, C)
                        for x, nx, y, ny in boxes
                    ],
                    0,
                )
                for a in range(3)
                for b in range(3)
            ],
            1,
        )
        product = dot(window, conv_flat[...])
        rows = (
            product[:, C : 2 * C]
            + shift_rows(product[:, :C], True)
            + shift_rows(product[:, 2 * C :], False)
        )
        active = (0.5 * rows * (1.0 + tanh_of(rows))).astype(BF16)
        done = 0
        for x, nx, y, ny in boxes:
            count = 16 * nx * ny
            shape = (nx, ny, 16, C)
            pre[pl.ds(x, nx), pl.ds(y, ny)] = rows[done : done + count].reshape(shape)
            hidden[pl.ds(x, nx), pl.ds(y, ny)] = active[done : done + count].reshape(shape)
            done += count

    convolve((1, 14, 1, 14))

    for copies in halos:
        copies.wait_recv()
    lm_first = scatter_rows(lm_part, lm_slots, sem_lm1, "grp")
    sides = (tile > 0, tile < TILE - 1, grp > 0, grp < GRP - 1)

    def keep(flag, rows):
        return jnp.where(flag, rows, jnp.zeros_like(rows))

    for side, x in ((0, 0), (1, 17)):
        rim[x, 1:17] = keep(sides[side], halo_x[side])
    for side, y in ((0, 0), (1, 17)):
        rim[1:17, y] = keep(sides[2 + side], halo_y[side])
    for i, x, y in ((0, 0, 0), (1, 0, 17), (2, 17, 0), (3, 17, 17)):
        flag = jnp.logical_and(sides[0 if x == 0 else 1], sides[2 if y == 0 else 3])
        rim[x, y] = keep(flag, halo_c[i])

    def windows():
        return jnp.concatenate(
            [rim[pl.ds(a, 16), b : b + 16].reshape(4096, C) for a in range(3) for b in range(3)], 1
        )

    convolve((0, 1, 0, 16), (15, 1, 0, 16), (1, 14, 0, 1), (1, 14, 15, 1))

    for i in range(8):
        total = hidden[2 * i].astype(F32) + hidden[2 * i + 1].astype(F32)
        coarse = (0.125 * pool(total.reshape(256, C), tmp)).astype(BF16)
        feats[pl.ds(64 * i, 64), pl.ds(0, C)] = coarse
        filter1[0][:, i] = dot(z_cells[...], coarse).astype(BF16).reshape(KZ, 16, C)

    def outer_grads():
        @pl.loop(0, 8)
        def _(i):
            total = cot[2 * i].astype(F32) * sea_of(2 * i)
            total += cot[2 * i + 1].astype(F32) * sea_of(2 * i + 1)
            rows = pool(total.reshape(256, C), tmp)
            proj_grad[pl.ds(pl.multiple_of(64 * i, 64), 64), :] = rows.astype(BF16)

        stacked[pl.ds(0, C), :] = lift[...]

    def back_through():
        for j in range(4):
            cols = pl.ds(256 * j, 256)
            bottle_grad[:, cols] = dot(proj_grad[...], proj[cols, :], 1, 1).astype(BF16)

    lm = {}

    def gather_lm():
        lm_mine[...] = add_rows(lm_part, lm_slots, lm_first, "grp")
        lm["grp"] = spread_rows(lm_mine, lm_all.at[core], sem_lm2, "grp")
        back_through()

    def swap_lm():
        lm["grp"].wait_recv()
        lm["core"] = to_partner(lm_all.at[core], lm_all.at[core], sem_lm3)

    def slopes():
        @pl.loop(0, 16)
        def _(x):
            value = pre[x].reshape(256, C)
            slope = gelu_slope(value, tanh_of(value))
            pre[x] = slope.reshape(16, 16, C)
            base[x] = slope * (cot[x].astype(F32) * sea_of(x)).reshape(256, C)

    x_filter(y_tab, x_tab, filter1, (outer_grads, gather_lm, slopes, swap_lm))

    lm["core"].wait_recv()
    for p in range(2):
        for j in range(GRP):
            stacked[pl.ds(C * (p + 1), C), pl.ds(C * j, C)] = lm_all[p, j]
    for copies in (lm_first, lm["grp"], lm["core"]):
        copies.wait_send()

    for i in range(8):
        modes = filter1[3][:, i].reshape(128, C)
        both = (SCALE * dot(z_twice[...], modes, 0, 0)).astype(BF16)
        feats[pl.ds(64 * i, 64), pl.ds(C, C)] = both[:64]
        feats[pl.ds(64 * i, 64), pl.ds(2 * C, C)] = both[64:]

    for j in range(4):
        cols = pl.ds(256 * j, 256)
        bottle_pre[...] = dot(feats[...], stacked[:, cols])

        @pl.loop(0, 8)
        def _(r):
            rows = pl.ds(pl.multiple_of(64 * r, 64), 64)
            v = bottle_pre[rows, :]
            t = tanh_of(v)
            bottle[rows, cols] = (0.5 * v * (1.0 + t)).astype(BF16)
            bpg[rows, cols] = (bottle_grad[rows, cols].astype(F32) * gelu_slope(v, t)).astype(BF16)

    feats_grad = dot(bpg[...], stacked[...], 1, 1)
    direct[...] = feats_grad[:, :C]
    pair_grad = (SCALE * feats_grad[:, C:]).astype(BF16)
    for i in range(8):
        rows = pair_grad[64 * i : 64 * (i + 1)]
        stacked_rows = jnp.concatenate([rows[:, :C], rows[:, C:]], 0)
        filter2[0][:, i] = dot(z_tab[...], stacked_rows).astype(BF16).reshape(KZ, 16, C)

    def weight_sums():
        for j in range(GRP):
            cols = pl.ds(C * j, C)
            outer = dot(feats[...], bpg[:, cols], 0, 0).astype(BF16)
            for k in range(3):
                rows = outer[C * k : C * (k + 1)]
                sums_in[block_at(8 * k + j)] = rows.reshape(8, 16, C)
            rows = dot(bottle[:, cols], proj_grad[...], 0, 0).astype(BF16)
            sums_in[block_at(24 + j)] = rows.reshape(8, 16, C)
        first_sums.run(0)

    def write_cells():
        direct_out = dot(bottle[...], proj[...])
        for i in range(8):
            cell_grad[i] = direct_out[64 * i : 64 * (i + 1)]

        @pl.loop(0, 8)
        def _(i):
            spread = unpool(cell_grad[i], tmp)
            for half in range(2):
                x = 2 * i + half
                value = hidden[x].astype(F32) + spread.reshape(16, 16, C)
                out[x] = (value * sea_of(x)).astype(BF16)

        stores[0].start()

    x_filter(
        y_tab,
        x_tab,
        filter2,
        (weight_sums, lambda: first_sums.run(1), write_cells, lambda: first_sums.run(2)),
    )

    for i in range(8):
        modes = filter2[3][:, i].reshape(128, C)
        rows = dot(z_twice[...], modes, 0, 0)[:64] + direct[pl.ds(64 * i, 64), :]
        cell_grad[i] = 0.125 * rows

    first_sums.run(3)

    @pl.loop(0, 8)
    def _(i):
        spread = unpool(cell_grad[i], tmp)
        for half in range(2):
            x = 2 * i + half
            grad = (base[x] + spread * pre[x].reshape(256, C)).astype(BF16).astype(F32)
            shifted = jnp.concatenate(
                [shift_rows(grad, False), grad, shift_rows(grad, True)], 1
            ).astype(BF16)
            upstream[:, pl.ds(pl.multiple_of(256 * x, 256), 256)] = shifted.T

    acc[...] = dot(upstream[...], windows()).astype(BF16)
    for c in range(3):
        for ab in range(9):
            rows = acc[pl.ds(C * c, C), pl.ds(C * ab, C)]
            taps_in[block_at(9 * c + ab)] = rows.reshape(8, 16, C)
    for n in range(27, 32):
        taps_in[block_at(n)] = jnp.zeros((8, 16, C), BF16)
    last_sums.run(0)
    first_sums.run(4)
    last_sums.run(1)
    first_sums.run(5)
    last_sums.run(2)
    first_sums.run(6)
    stores[1].start()
    last_sums.run(3)

    total = jnp.zeros((C, C), F32)
    for p in range(2):
        for j in range(GRP):
            cols = pl.ds(C * j, C)
            grads = sums[block_at(8 * (1 + p) + j)].reshape(C, C)
            total += dot(grads, mix[p, :, cols], 1, 1)
    lift_mine[...] = total.astype(BF16)
    lift_copies = spread_rows(lift_mine, lift_parts, sem_lift, "grp")
    last_sums.run(4)
    lift_copies.wait_recv()
    stores[2].start()
    for copies in (lift_copies, *halos):
        copies.wait_send()
    last_sums.run(5)
    stores[3].start()
    last_sums.run(6)
    for copy in stores:
        copy.wait()


def finish_kernel(
    out_in,
    sums_in,
    taps_in,
    parts_in,
    lift_in,
    out_to,
    conv_to,
    lift_to,
    mix_to,
    proj_to,
    out,
    sums,
    taps,
    parts,
    own_rows,
    conv,
    lift,
    mix,
    proj,
    sems,
):
    def copies(first, *pairs):
        return [
            pltpu.make_async_copy(src, dst, sems.at[first + i])
            for i, (src, dst) in enumerate(pairs)
        ]

    cols = pl.ds(pl.multiple_of(spot("grp") * C, C), C)
    loads = copies(
        0,
        (taps_in, taps),
        (sums_in, sums),
        (parts_in, parts),
        (lift_in.at[:, cols], own_rows),
        (out_in, out),
    )
    stores = copies(5, (conv, conv_to), (lift, lift_to), (mix, mix_to), (proj, proj_to), (out, out_to))
    for copy in loads:
        copy.start()
    loads[0].wait()
    for c in range(3):
        for ab in range(9):
            conv[3 * ab + c] = taps[9 * c + ab].astype(F32).T
    stores[0].start()
    for copy in loads[1:4]:
        copy.wait()
    for j in range(GRP):
        cols = pl.ds(C * j, C)
        lift[:, cols] = sums[j].astype(F32) + parts[j].astype(F32)
        proj[j] = sums[24 + j].astype(F32)
        for p in range(2):
            mix[p, :, cols] = dot(own_rows[...], sums[8 * (1 + p) + j], 0, 0)
    for copy in stores[1:4]:
        copy.start()
    loads[4].wait()
    stores[4].start()
    for copy in stores:
        copy.wait()


def shards(
    field,
    sea,
    conv_weight,
    lift_weight,
    mix_weight,
    proj_weight,
    kx_modes,
    ky_modes,
    kz_modes,
    cotangent,
):
    smem = pl.BlockSpec(memory_space=pltpu.SMEM)
    hbm = pl.BlockSpec(memory_space=pl.ANY)
    out, sums, taps, lift_parts = pl.pallas_call(
        step_kernel,
        out_shape=(
            jax.ShapeDtypeStruct(field.shape, BF16),
            jax.ShapeDtypeStruct((2, 2, 4, 16, 16, C), BF16),
            jax.ShapeDtypeStruct((2, 2, 4, 16, 16, C), BF16),
            jax.ShapeDtypeStruct((GRP, C, C), BF16),
        ),
        in_specs=[hbm] * 7 + [smem] * 3,
        out_specs=(hbm,) * 4,
        scratch_shapes=[
            held(16, 16, 16, C),
            pltpu.VMEM((16, 16, 16), jnp.int32),
            held(4096, C, dtype=F32),
            held(16, 16, 16, C),
            held(3, 3, 3, C, C),
            held(C, W),
            held(2, C, W),
            held(W, C),
            pltpu.SemaphoreType.DMA((7,)),
            held(64, 256),
            held(32, 128),
            held(64, 128),
            held(64, 64),
            held(128, 128),
            held(18, 18, 16, C),
            held(3 * C, 4096),
            held(2, 16, 16, C),
            held(2, 16, 16, C),
            held(4, 16, C),
            held(9 * C, 3 * C),
            held(16, 16, 16, C, dtype=F32),
            held(16, 256, C, dtype=F32),
            held(16, 16, 16, C),
            held(512, 3 * C),
            held(512, C),
            held(C, C),
            held(GRP, C, C),
            held(GRP, C, C),
            held(C, C),
            held(2, GRP, C, C),
            held(3 * C, W),
            held(512, 256, dtype=F32),
            held(512, W),
            held(512, W),
            held(512, W),
            held(512, C, dtype=F32),
            held(8, 64, C, dtype=F32),
            held(3 * C, 9 * C),
            held(2, 2, 4, 16, 16, C),
            held(2, 2, 4, 16, 16, C),
            held(C, C),
            held(128, C, dtype=F32),
            held(16, 16, 16, C),
            held(2, 2, 4, 16, 16, C),
            held(2, 2, 4, 16, 16, C),
            held(GRP, C, C),
            pltpu.SemaphoreType.DMA((4,)),
            pltpu.SemaphoreType.DMA((3, 2)),
            pair_sems(),
            pair_sems(),
            pair_sems(),
            pair_sems(),
        ]
        + FILTER_SCRATCH()
        + FILTER_SCRATCH()
        + SUM_SCRATCH()
        + SUM_SCRATCH(),
        compiler_params=pltpu.CompilerParams(
            collective_id=1, has_side_effects=True, vmem_limit_bytes=56 * 2**20
        ),
        name="step",
    )(
        field,
        sea,
        cotangent,
        conv_weight,
        lift_weight,
        mix_weight,
        proj_weight,
        kx_modes,
        ky_modes,
        kz_modes,
    )
    out, conv, lift, mix, proj = pl.pallas_call(
        finish_kernel,
        out_shape=(
            jax.ShapeDtypeStruct(field.shape, BF16),
            jax.ShapeDtypeStruct((27, C, C), F32),
            jax.ShapeDtypeStruct((C, W), F32),
            jax.ShapeDtypeStruct((2, C, W), F32),
            jax.ShapeDtypeStruct((GRP, C, C), F32),
        ),
        in_specs=[hbm] * 5,
        out_specs=(hbm,) * 5,
        scratch_shapes=[
            held(16, 16, 16, C),
            held(32, C, C),
            held(32, C, C),
            held(GRP, C, C),
            held(C, C),
            held(27, C, C, dtype=F32),
            held(C, W, dtype=F32),
            held(2, C, W, dtype=F32),
            held(GRP, C, C, dtype=F32),
            pltpu.SemaphoreType.DMA((10,)),
        ],
        compiler_params=pltpu.CompilerParams(vmem_limit_bytes=56 * 2**20),
        name="finish",
    )(out, sums.reshape(32, C, C), taps.reshape(32, C, C), lift_parts, lift_weight)
    return (out, conv.reshape(3, 3, 3, C, C), lift, mix, proj.reshape(W, C))


def solution(mesh):
    return jax.shard_map(
        shards,
        mesh=mesh,
        in_specs=(
            P("tile", "grp", None, None),
            P("tile", "grp", None),
            P(),
            P(),
            P(None, "grp", None),
            P(),
            P(),
            P(),
            P(),
            P("tile", "grp", None, None),
        ),
        out_specs=(P("tile", "grp", None, None), P(), P(), P(None, "grp", None), P()),
        check_vma=False,
    )
```
